512 devices in a mesh: date: 32 (over y_hi, z), row: 8 (over x, core), col: 2 (over y_lo).
Axes of the slice: x: 4, y: 4 (y_hi: 2, y_lo: 2; y = y_hi * 2 + y_lo), z: 16, core: 2. Of those that a mesh axis runs over, the one named last changes fastest.
Arguments:
- images: float32 [64, 2, 384, 1536], P('date', None, 'row', 'col'), may hold values from -8 to 8
- secondaries: int32 [64, 3], P('date'), may hold values from 0 to 63, as said below
Outputs:
- filtered: float32 [64, 3, 2, 192, 192], P('date', None, None, 'row', 'col')
- coherence: float32 [64, 3, 2, 192, 192], P('date', None, None, 'row', 'col')
The draws below stay inside these ranges and needn't reach their ends.
Inputs may be any that keep to these rules, and one draw needn't show every extreme that they name: secondaries[k, l] = (k + o) mod 64 for 3 distinct offsets o of 1 to 4, rising with l; the offset 4 occurs in every draw.
All inputs are finite; a program needn't handle non-finite values.
Results may differ from the reference program's by a relative error of at most 0.00005.
Values sent between devices are 32-bit elements; how exact they have to be, the bound alone decides.
No kernel may reach another device: no remote copies, remote signals or barrier semaphores. Data moves between devices by JAX's collectives and lax.ppermute only.
A program may use at most 128 MiB of HBM per device.

```python
import math
import jax
import jax.numpy as jnp
from jax import lax

LINKS = 3
REACH = 4
LOOK_R = 2
LOOK_C = 8
PATCH = 32
KEEP = 24
MARGIN = 4
DATES = 64
ROWS = 384
COLS = 1536


def draw_images(key, part):
    key = jax.random.fold_in(key, 11)
    subkeys = jax.random.split(key, 5)
    scene = jnp.clip(jax.random.normal(subkeys[0], (2, ROWS, COLS), jnp.float32), -4.0, 4.0)
    rate_rows = jax.random.uniform(subkeys[1], (DATES, 1, 1), jnp.float32, -0.3, 0.3)
    rate_cols = jax.random.uniform(subkeys[2], (DATES, 1, 1), jnp.float32, -0.05, 0.05)
    offset = jax.random.uniform(subkeys[3], (DATES, 1, 1), jnp.float32, -math.pi, math.pi)
    row_axis = jnp.arange(ROWS, dtype=jnp.float32)[None, :, None]
    col_axis = jnp.arange(COLS, dtype=jnp.float32)[None, None, :]
    phases = rate_rows * row_axis + rate_cols * col_axis + offset
    noise = jnp.clip(jax.random.normal(subkeys[4], (DATES, 2, ROWS, COLS), jnp.float32), -4.0, 4.0)
    amplitude = jnp.ones((1, ROWS, 1), jnp.float32)
    cosine = jnp.cos(phases)
    sine = jnp.sin(phases)
    real_part = 0.8 * amplitude * (scene[0] * cosine - scene[1] * sine) + 0.6 * noise[:, 0]
    imag_part = 0.8 * amplitude * (scene[0] * sine + scene[1] * cosine) + 0.6 * noise[:, 1]
    return jnp.clip(jnp.stack([real_part, imag_part], axis=1), -8.0, 8.0)


def draw_secondaries(key, part):
    key = jax.random.fold_in(key, 23)
    dropped = jax.random.randint(key, (DATES,), 1, REACH + 1)
    date_ids = jnp.arange(DATES, dtype=jnp.int32)
    dropped = jnp.where(date_ids == 0, 1, dropped).astype(jnp.int32)
    counter = jnp.arange(1, LINKS + 1, dtype=jnp.int32)[None, :]
    offsets = counter + (counter >= dropped[:, None]).astype(jnp.int32)
    return ((date_ids[:, None] + offsets) % DATES).astype(jnp.int32)


def setup_inputs(seed: int = 0) -> dict:
    splits = jax.random.split(jax.random.key(seed), 3)
    images = draw_images(jax.random.fold_in(splits[2], 71), 0)
    secondaries = draw_secondaries(jax.random.fold_in(splits[2], 71), 0)
    return {"images": images, "secondaries": secondaries}


def multilook(values):
    extent = values.shape
    blocks = values.reshape(extent[:-2] + (extent[-2] // LOOK_R, LOOK_R, extent[-1] // LOOK_C, LOOK_C))
    return blocks.mean(axis=(-3, -1))

def window_last(grid_values, block_count):
    leading = grid_values.shape[:-1]
    head_part = grid_values[..., :block_count * KEEP].reshape(leading + (block_count, KEEP))
    widths = [(0, 0)] * (grid_values.ndim - 1) + [(0, 2 * KEEP - PATCH)]
    extended = jnp.pad(grid_values, widths)
    tail_part = extended[..., KEEP:].reshape(leading + (block_count, KEEP))[..., :PATCH - KEEP]
    return jnp.concatenate([head_part, tail_part], axis=-1)

def patches(grid_values, row_blocks, col_blocks):
    across = window_last(grid_values, col_blocks)
    turned = jnp.moveaxis(across, -3, -1)
    stacked = window_last(turned, row_blocks)
    return jnp.moveaxis(stacked, (-4, -3), (-2, -1))

def box_mean(padded, rows_out, cols_out):
    summed = jnp.zeros(padded.shape[:-2] + (rows_out, cols_out), padded.dtype)
    for row_step in (-1, 0, 1):
        for col_step in (-1, 0, 1):
            summed = summed + padded[..., MARGIN + row_step:MARGIN + row_step + rows_out, MARGIN + col_step:MARGIN + col_step + cols_out]
    return summed / 9.0

def coherence_from(real_pad, imag_pad, first_pad, second_pad, rows_out, cols_out):
    cross_real = box_mean(real_pad, rows_out, cols_out)
    cross_imag = box_mean(imag_pad, rows_out, cols_out)
    energy = box_mean(first_pad, rows_out, cols_out) * box_mean(second_pad, rows_out, cols_out)
    factor = lax.rsqrt(energy + 1e-06)
    return jnp.stack([cross_real * factor, cross_imag * factor], axis=-3)

def weights_of(power):
    smooth = jnp.zeros_like(power)
    for row_step in (-1, 0, 1):
        for col_step in (-1, 0, 1):
            smooth = smooth + jnp.roll(power, (row_step, col_step), axis=(-3, -1))
    smooth = smooth / 9.0
    level = lax.optimization_barrier(jnp.mean(power, axis=(-3, -1), keepdims=True))
    weight = (smooth + level + 1e-06) ** 0.25
    return weight / lax.optimization_barrier(jnp.mean(weight, axis=(-3, -1), keepdims=True))

def centre(values, row_blocks, col_blocks):
    kept = values[..., MARGIN:MARGIN + KEEP, :, MARGIN:MARGIN + KEEP]
    return kept.reshape(kept.shape[:-4] + (row_blocks * KEEP, col_blocks * KEEP))

def goldstein(real_pad, imag_pad, row_blocks, col_blocks):
    field = patches(real_pad, row_blocks, col_blocks) + 1j * patches(imag_pad, row_blocks, col_blocks)
    spectrum = jnp.fft.fft2(field, axes=(-3, -1))
    power = jnp.real(spectrum) ** 2 + jnp.imag(spectrum) ** 2
    result = jnp.fft.ifft2(spectrum * weights_of(power), axes=(-3, -1))
    return jnp.stack([centre(jnp.real(result), row_blocks, col_blocks), centre(jnp.imag(result), row_blocks, col_blocks)], axis=-3)

def reference(images, secondaries):
    rows_out = ROWS // LOOK_R
    cols_out = COLS // LOOK_C
    row_blocks = rows_out // KEEP
    col_blocks = cols_out // KEEP

    def widen(values):
        return jnp.pad(values, [(0, 0)] * (values.ndim - 2) + [(MARGIN, MARGIN), (MARGIN, MARGIN)])

    def one_date(entry):
        index, second_dates = entry
        own_date = lax.dynamic_index_in_dim(images, index, 0, keepdims=False)
        partners = jnp.take(images, second_dates, axis=0)
        pair_real = multilook(own_date[0] * partners[:, 0] + own_date[1] * partners[:, 1])
        pair_imag = multilook(own_date[1] * partners[:, 0] - own_date[0] * partners[:, 1])
        first_power = multilook(own_date[0] ** 2 + own_date[1] ** 2)[None]
        second_power = multilook(partners[:, 0] ** 2 + partners[:, 1] ** 2)
        real_pad = widen(pair_real)
        imag_pad = widen(pair_imag)
        coherent = coherence_from(real_pad, imag_pad, widen(first_power), widen(second_power), rows_out, cols_out)
        filtered = goldstein(real_pad, imag_pad, row_blocks, col_blocks)
        return (filtered, coherent)
    filtered, coherent = lax.map(one_date, (jnp.arange(DATES, dtype=jnp.int32), secondaries))
    return (filtered, coherent)
```

```python
import functools
import math

import jax
import jax.numpy as jnp
import numpy as np
from jax import lax
from jax.experimental import pallas as pl
from jax.experimental.pallas import tpu as pltpu
from jax.sharding import PartitionSpec as P

KEEP = 24
PATCH = 32
MARGIN = 4
LANES = 128
STRIP = 32
LINKS = 3
F32 = jnp.float32
BF16 = jnp.bfloat16

HELD = ((0, 1), (0, 2), (0, 3), (1, 2), (1, 3))
SENT = ((-2, 2), (-1, 2), (-1, 3))


def vmem():
    return pl.BlockSpec(memory_space=pltpu.VMEM)


def smem():
    return pl.BlockSpec(memory_space=pltpu.SMEM)


def call(kernel, outs, count, scratch=(), specs=None, flops=1e6, moved=1e6):
    return pl.pallas_call(
        kernel,
        out_shape=outs,
        in_specs=specs or [vmem()] * count,
        out_specs=jax.tree.map(lambda _: vmem(), outs),
        scratch_shapes=list(scratch),
        compiler_params=pltpu.CompilerParams(vmem_limit_bytes=32 * 1024 * 1024),
        cost_estimate=pl.CostEstimate(flops=int(flops), bytes_accessed=int(moved), transcendentals=0),
    )


def lane_index(shape):
    return lax.broadcasted_iota(jnp.int32, shape, len(shape) - 1)


def edge_kernel(first_ref, last_ref, out_ref):
    at_left = lax.axis_index("col") == 0
    lanes = lane_index(first_ref.shape[2:])
    for part in range(2):
        pieces = []
        for date in range(2):
            left = first_ref[date, part]
            right = pltpu.roll(last_ref[date, part], STRIP, 1)
            pieces.append(jnp.where(at_left, right, left))
        zero, one = pieces
        value = jnp.where(lanes < STRIP, zero, pltpu.roll(one, STRIP, 1))
        value = jnp.where(lanes < 2 * STRIP, value, pltpu.roll(zero, 2 * STRIP, 1))
        value = jnp.where(lanes < 3 * STRIP, value, pltpu.roll(one, 3 * STRIP, 1))
        out_ref[part] = value


def edge_of(images):
    rows, cols = images.shape[2:]
    spec = lambda index: pl.BlockSpec((2, 2, rows, LANES), lambda i: (0, 0, 0, index))
    return pl.pallas_call(
        edge_kernel,
        grid=(1,),
        out_shape=jax.ShapeDtypeStruct((2, rows, LANES), F32),
        in_specs=[spec(0), spec(cols // LANES - 1)],
        out_specs=pl.BlockSpec((2, rows, LANES), lambda i: (0, 0, 0)),
    )(images, images)


def looks_table(cols, at_left):
    shape = (cols, LANES)
    source = lax.broadcasted_iota(jnp.int32, shape, 0)
    target = lax.broadcasted_iota(jnp.int32, shape, 1)
    main = jnp.where((source >> 3) + MARGIN == target, 1.0 / 16.0, 0.0)
    shape = (LANES, LANES)
    source = lax.broadcasted_iota(jnp.int32, shape, 0)
    target = lax.broadcasted_iota(jnp.int32, shape, 1)
    place = jnp.where(at_left, MARGIN + cols // 8, 0)
    edge = jnp.where(((source & (STRIP - 1)) >> 3) + place == target, 1.0 / 16.0, 0.0)
    return jnp.concatenate([main, edge], axis=0).astype(BF16)


def split_dot(values, table):
    high = values.astype(BF16)
    rest = values - high.astype(F32)
    middle = rest.astype(BF16)
    low = (rest - middle.astype(F32)).astype(BF16)
    dot = lambda v: jnp.dot(v, table, preferred_element_type=F32)
    return dot(high) + (dot(middle) + dot(low))


def pairs_kernel(*refs):
    own_edge, after_edge, before_edge, held, sent, stage = refs[-6:]
    tiles = (len(refs) - 6) // 3
    own, after, before = refs[:tiles], refs[tiles : 2 * tiles], refs[2 * tiles : 3 * tiles]
    cols = tiles * LANES
    half = own_edge.shape[1] // 2
    at_left = lax.axis_index("col") == 0
    holders = {-2: (before, 0), -1: (before, 1), 0: (own, 0), 1: (own, 1), 2: (after, 0), 3: (after, 1)}

    def image(slot, tile):
        refs, date = holders[slot]
        return [
            [refs[tile][date, part, pl.ds(parity, half, stride=2), :] for parity in range(2)]
            for part in range(2)
        ]

    def edge(ref):
        return [[ref[part, pl.ds(parity, half, stride=2), :] for parity in range(2)] for part in range(2)]

    def product(a, b):
        (ar, ai), (br, bi) = a, b
        real = (ar[0] * br[0] + ai[0] * bi[0]) + (ar[1] * br[1] + ai[1] * bi[1])
        imag = (ai[0] * br[0] - ar[0] * bi[0]) + (ai[1] * br[1] - ar[1] * bi[1])
        return real, imag

    def power(a):
        ar, ai = a
        return (ar[0] * ar[0] + ai[0] * ai[0]) + (ar[1] * ar[1] + ai[1] * ai[1])

    pairs = HELD + SENT
    planes = 2 * len(pairs)
    for tile in range(tiles):
        lanes = pl.ds(tile * LANES, LANES)
        loaded = {slot: image(slot, tile) for slot in holders}
        for n, (a, b) in enumerate(pairs):
            real, imag = product(loaded[a], loaded[b])
            stage[pl.ds(2 * n * half, half), lanes] = real
            stage[pl.ds((2 * n + 1) * half, half), lanes] = imag
        for slot in range(4):
            stage[pl.ds((planes + slot) * half, half), lanes] = power(loaded[slot])

    lanes = pl.ds(cols, LANES)
    block = lane_index((half, LANES)) >> 5

    def only(value, wanted):
        return jnp.where(block == wanted, value, 0.0)

    turned = lambda a: [[pltpu.roll(v, STRIP, 1) for v in part] for part in a]
    mine, theirs, earlier = edge(own_edge), edge(after_edge), edge(before_edge)
    crossed = [
        [jnp.where(block < 2, v, w) for v, w in zip(p, q)] for p, q in zip(theirs, turned(theirs))
    ]
    local = product(mine, turned(mine))
    ahead = product(mine, crossed)
    met = product(earlier, crossed)
    where = {
        (0, 1): (local, 0),
        (0, 2): (ahead, 0),
        (1, 3): (ahead, 1),
        (0, 3): (ahead, 2),
        (1, 2): (ahead, 3),
        (-2, 2): (met, 0),
        (-1, 3): (met, 1),
        (-1, 2): (met, 3),
    }
    for n, pair in enumerate(pairs):
        (real, imag), wanted = where[pair]
        stage[pl.ds(2 * n * half, half), lanes] = only(real, wanted)
        stage[pl.ds((2 * n + 1) * half, half), lanes] = only(imag, wanted)
    own_power, after_power = power(mine), power(theirs)
    for slot in range(4):
        value = own_power if slot < 2 else after_power
        stage[pl.ds((planes + slot) * half, half), lanes] = only(value, slot % 2)

    means = split_dot(stage[...], looks_table(cols, at_left))
    split = 2 * len(HELD) * half
    end = planes * half
    held[pl.ds(0, split), :] = means[:split]
    held[pl.ds(split, 4 * half), :] = means[end:]
    sent[pl.ds(0, end - split), :] = means[split:end]
    sent[pl.ds(end - split, 2 * half), :] = means[end + 2 * half :]


def pairs_of(own, after, before, own_edge, after_edge, before_edge):
    rows, cols = own.shape[2:]
    half, tiles = rows // 2, cols // LANES
    tile = lambda index: pl.BlockSpec((2, 2, rows, LANES), lambda i: (0, 0, 0, index))
    edge = pl.BlockSpec((2, rows, LANES), lambda i: (0, 0, 0))
    plane = lambda count: jax.ShapeDtypeStruct((count * half, LANES), F32)
    whole = lambda out: pl.BlockSpec(out.shape, lambda i: (0, 0))
    total = 2 * len(HELD + SENT) + 4
    outs = (plane(2 * len(HELD) + 4), plane(2 * len(SENT) + 2))
    return pl.pallas_call(
        pairs_kernel,
        grid=(1,),
        out_shape=outs,
        in_specs=[tile(index) for index in range(tiles)] * 3 + [edge] * 3,
        out_specs=tuple(whole(out) for out in outs),
        scratch_shapes=[pltpu.VMEM((total * half, cols + LANES), F32)],
        compiler_params=pltpu.CompilerParams(vmem_limit_bytes=32 * 1024 * 1024),
    )(*[own] * tiles, *[after] * tiles, *[before] * tiles, own_edge, after_edge, before_edge)


def chosen(secondaries, held, back, all_planes):
    size = KEEP
    order = [("h", 0), ("h", 1), ("h", 2), ("b", 0), ("h", 3), ("h", 4), ("b", 1), ("b", 2)]
    for n, (which, index) in enumerate(order):
        ref = held if which == "h" else back
        all_planes[pl.ds(2 * n * size, 2 * size), :] = ref[pl.ds(2 * index * size, 2 * size), :]
    base = 2 * len(order) * size
    all_planes[pl.ds(base, 4 * size), :] = held[pl.ds(2 * len(HELD) * size, 4 * size), :]
    all_planes[pl.ds(base + 4 * size, 2 * size), :] = back[pl.ds(2 * len(SENT) * size, 2 * size), :]
    first = 2 * lax.axis_index("date")
    dates = 2 * lax.axis_size("date")

    def planes(date, link):
        slot = (secondaries[date, link] - first + dates) % dates
        pair = 4 * date + slot - 1 - date
        starts = (2 * pair, 2 * pair + 1, 16 + date, 16 + slot)
        return [pl.multiple_of(s * size, 8) if not isinstance(s, int) else s * size for s in starts]

    return planes


def rims_kernel(secondaries, held, back, chip, across, all_planes):
    planes = chosen(secondaries, held, back, all_planes)
    even = lax.axis_index("row") % 2 == 0
    n = 0
    for date in range(2):
        for link in range(LINKS):
            for start in planes(date, link):
                top = all_planes[pl.ds(start, 8), :]
                bottom = pltpu.roll(all_planes[pl.ds(start + KEEP - 8, 8), :], 4, 0)
                chip[pl.ds(4 * n, 4), :] = jnp.where(even, bottom, top)[:4]
                across[pl.ds(4 * n, 4), :] = jnp.where(even, top, bottom)[:4]
                n += 1


@functools.lru_cache(None)
def tables():
    blocks = LANES // PATCH
    n = np.arange(PATCH)
    angle = 2.0 * np.pi * (np.outer(n, n) % PATCH) / PATCH
    cosine, sine = np.cos(angle), np.sin(angle)
    forward = np.zeros((LANES, 2 * LANES))
    spread = np.zeros((LANES, 2 * LANES))
    inverse = np.zeros((LANES, 2 * LANES))
    for b in range(blocks):
        f = slice(b * PATCH, (b + 1) * PATCH)
        x = slice(b * KEEP, b * KEEP + PATCH)
        o = slice(b * KEEP, (b + 1) * KEEP)
        kept = slice(MARGIN, MARGIN + KEEP)
        forward[x, f] = cosine
        forward[x, LANES + b * PATCH : LANES + (b + 1) * PATCH] = -sine
        inverse[f, o] = cosine[:, kept] / PATCH
        inverse[f, LANES + b * KEEP : LANES + (b + 1) * KEEP] = sine[:, kept] / PATCH
        near = (n[:, None] - n[None, :]) % PATCH
        spread[f, f] = (near == 0) | (near == 1) | (near == PATCH - 1)
        spread[f, LANES + b * PATCH : LANES + (b + 1) * PATCH] = 1.0
    down = np.block([[cosine, sine], [-sine, cosine]])
    kept = slice(MARGIN, MARGIN + KEEP)
    up = np.block([[cosine[kept], -sine[kept]], [sine[kept], cosine[kept]]]) / PATCH
    return [np.asarray(t, np.float32) for t in (forward, spread, inverse, down, up)]


def exact_dot(a, b):
    return jnp.dot(a, b, preferred_element_type=F32, precision=lax.Precision.HIGHEST)


def filter_kernel(
    secondaries, held, back, chip, across, forward, spread, inverse, down, up, filtered, coherent, all_planes, pad
):
    planes = chosen(secondaries, held, back, all_planes)
    even = lax.axis_index("row") % 2 == 0
    pairs = 2 * LINKS
    n = 0
    for date in range(2):
        for link in range(LINKS):
            for start in planes(date, link):
                near, far = chip[pl.ds(4 * n, 4), :], across[pl.ds(4 * n, 4), :]
                pad[n, pl.ds(0, 4), :] = jnp.where(even, far, near)
                pad[n, pl.ds(4, KEEP), :] = all_planes[pl.ds(start, KEEP), :]
                pad[n, pl.ds(4 + KEEP, 4), :] = jnp.where(even, near, far)
                n += 1

    def box(value):
        rows = value[3 : 3 + KEEP] + value[4 : 4 + KEEP] + value[5 : 5 + KEEP]
        total = pltpu.roll(rows, LANES - 3, 1) + pltpu.roll(rows, LANES - 4, 1) + pltpu.roll(rows, LANES - 5, 1)
        return total * (1.0 / 9.0)

    wide = coherent.shape[-1]
    for p in range(pairs):
        real, imag, first, second = [box(pad[4 * p + k]) for k in range(4)]
        factor = lax.rsqrt(first * second + 1e-06)
        coherent[p // LINKS, p % LINKS, 0] = (real * factor)[:, :wide]
        coherent[p // LINKS, p % LINKS, 1] = (imag * factor)[:, :wide]

    reals = jnp.concatenate([pad[4 * p] for p in range(pairs)], axis=0)
    imags = jnp.concatenate([pad[4 * p + 1] for p in range(pairs)], axis=0)
    size = pairs * PATCH
    across_cols = exact_dot(jnp.concatenate([reals, imags], axis=0), forward[...])
    col_real = across_cols[:size, :LANES] - across_cols[size:, LANES:]
    col_imag = across_cols[size:, :LANES] + across_cols[:size, LANES:]
    rows_of = lambda v, p, count: v[p * count : (p + 1) * count]
    stacked = jnp.concatenate(
        [
            jnp.concatenate([rows_of(col_real, p, PATCH), rows_of(col_imag, p, PATCH)], axis=0)
            for p in range(pairs)
        ],
        axis=1,
    )
    spectrum = exact_dot(down[...], stacked)
    real, imag = spectrum[:PATCH], spectrum[PATCH:]
    power = real * real + imag * imag
    lanes_of = lambda v, p: v[:, p * LANES : (p + 1) * LANES]
    tall = lambda v: jnp.concatenate([lanes_of(v, p) for p in range(pairs)], axis=0)
    sums = exact_dot(tall(power), spread[...])
    weights = []
    for p in range(pairs):
        near = rows_of(sums, p, PATCH)[:, :LANES]
        level = jnp.sum(rows_of(sums, p, PATCH)[:, LANES:], axis=0, keepdims=True) * (1.0 / (PATCH * PATCH))
        smooth = (near + pltpu.roll(near, 1, 0) + pltpu.roll(near, PATCH - 1, 0)) * (1.0 / 9.0)
        weights.append(jnp.sqrt(jnp.sqrt(smooth + level + 1e-06)))
    totals = exact_dot(jnp.concatenate(weights, axis=0), spread[:, LANES:])
    scaled = []
    for p in range(pairs):
        total = jnp.sum(rows_of(totals, p, PATCH), axis=0, keepdims=True)
        scaled.append(weights[p] * ((PATCH * PATCH) / total))
    weight = jnp.concatenate(scaled, axis=1)
    lifted = exact_dot(up[...], jnp.concatenate([real * weight, imag * weight], axis=0))
    low, high = lifted[:KEEP], lifted[KEEP:]
    size = pairs * KEEP
    result = exact_dot(jnp.concatenate([tall(low), tall(high)], axis=0), inverse[...])
    out_real = result[:size, :LANES] - result[size:, LANES:]
    out_imag = result[size:, :LANES] + result[:size, LANES:]
    for p in range(pairs):
        filtered[p // LINKS, p % LINKS, 0] = rows_of(out_real, p, KEEP)[:, :wide]
        filtered[p // LINKS, p % LINKS, 1] = rows_of(out_imag, p, KEEP)[:, :wide]


def shifted(value, axis, steps):
    count = lax.axis_size(axis)
    pairs = [(source, (source + steps) % count) for source in range(count)]
    return lax.ppermute(value, axis, pairs)


def body(images, secondaries):
    rows, cols = images.shape[2:]
    cells_down, cells_along = rows // 2, cols // 8
    rim = jax.ShapeDtypeStruct((2 * LINKS * 4 * MARGIN, LANES), F32)
    count = lax.axis_size("row")
    inside = [(i, i ^ 1) for i in range(count)]
    outside = [(i, ((i + 1) ^ 1) - 1) for i in range(1, count - 1)]

    after = shifted(images, "date", -1)
    before = shifted(images, "date", 1)
    edge = lax.ppermute(edge_of(images), "col", [(0, 1), (1, 0)])
    after_edge = shifted(edge, "date", -1)
    before_edge = shifted(edge, "date", 1)

    held, sent = pairs_of(images, after, before, edge, after_edge, before_edge)
    back = shifted(sent, "date", -1)

    every = pltpu.VMEM((22 * cells_down, LANES), F32)
    chip, across = call(rims_kernel, (rim, rim), 3, [every], [smem(), vmem(), vmem()])(secondaries, held, back)
    chip = lax.ppermute(chip, "row", inside)
    across = lax.ppermute(across, "row", outside)
    out = jax.ShapeDtypeStruct((2, LINKS, 2, cells_down, cells_along), F32)
    return call(
        filter_kernel,
        (out, out),
        10,
        [every, pltpu.VMEM((8 * LINKS, PATCH, LANES), F32)],
        [smem()] + [vmem()] * 9,
    )(secondaries, held, back, chip, across, *tables())


def solution(mesh):
    in_specs = (P("date", None, "row", "col"), P("date", None))
    out_specs = (P("date", None, None, "row", "col"), P("date", None, None, "row", "col"))
    return jax.shard_map(body, mesh=mesh, in_specs=in_specs, out_specs=out_specs, check_vma=False)
```

```python
import functools
import math

import jax
import jax.numpy as jnp
import numpy as np
from jax import lax
from jax.experimental import pallas as pl
from jax.experimental.pallas import tpu as pltpu
from jax.sharding import PartitionSpec as P

KEEP = 24
PATCH = 32
MARGIN = 4
LANES = 128
STRIP = 32
RIGHT = 100
LINKS = 3
RUN = 16
F32 = jnp.float32
BF16 = jnp.bfloat16

HELD = ((0, 1), (0, 2), (0, 3), (1, 2), (1, 3))
SENT = ((-2, 2), (-1, 2), (-1, 3))
CANDIDATES = tuple((a - 2, b - 2) for a in range(2) for b in range(a + 1, a + 5))
PLANES = 2 * len(CANDIDATES) + 6


def vmem():
    return pl.BlockSpec(memory_space=pltpu.VMEM)


def smem():
    return pl.BlockSpec(memory_space=pltpu.SMEM)


def call(kernel, outs, count, scratch=(), specs=None, flops=1e6, moved=1e6):
    return pl.pallas_call(
        kernel,
        out_shape=outs,
        in_specs=specs or [vmem()] * count,
        out_specs=jax.tree.map(lambda _: vmem(), outs),
        scratch_shapes=list(scratch),
        compiler_params=pltpu.CompilerParams(vmem_limit_bytes=32 * 1024 * 1024),
        cost_estimate=pl.CostEstimate(flops=int(flops), bytes_accessed=int(moved), transcendentals=0),
    )


def lane_index(shape):
    return lax.broadcasted_iota(jnp.int32, shape, len(shape) - 1)


def looks_table(cols):
    source = lax.broadcasted_iota(jnp.int32, (cols, LANES), 0)
    target = lax.broadcasted_iota(jnp.int32, (cols, LANES), 1)
    return jnp.where((source >> 3) + MARGIN == target, 1.0 / 16.0, 0.0).astype(BF16)


def split_dot(values, table):
    high = values.astype(BF16)
    rest = values - high.astype(F32)
    middle = rest.astype(BF16)
    low = (rest - middle.astype(F32)).astype(BF16)
    dot = lambda v: jnp.dot(v, table, preferred_element_type=F32)
    return dot(high) + (dot(middle) + dot(low))


def tiled(images):
    rows, cols = images.shape[2:]
    spec = lambda index: pl.BlockSpec((2, 2, rows, LANES), lambda i: (0, 0, 0, index))
    return [spec(index) for index in range(cols // LANES)]


def keep_kernel(source, target, arrived):
    copies = [
        pltpu.make_async_copy(
            source.at[:, :, :, pl.ds(tile * LANES, LANES)], target.at[tile], arrived.at[tile]
        )
        for tile in range(target.shape[0])
    ]
    for copy in copies:
        copy.start()
    for copy in copies:
        copy.wait()


def kept(images):
    tiles = images.shape[3] // LANES
    return pl.pallas_call(
        keep_kernel,
        out_shape=pltpu.VMEM((tiles,) + images.shape[:3] + (LANES,), F32),
        in_specs=[pl.BlockSpec(memory_space=pl.ANY)],
        out_specs=vmem(),
        scratch_shapes=[pltpu.SemaphoreType.DMA((tiles,))],
    )(images)


def product(a, b):
    (ar, ai), (br, bi) = a, b
    real = (ar[0] * br[0] + ai[0] * bi[0]) + (ar[1] * br[1] + ai[1] * bi[1])
    imag = (ai[0] * br[0] - ar[0] * bi[0]) + (ai[1] * br[1] - ar[1] * bi[1])
    return real, imag


def power(a):
    ar, ai = a
    return (ar[0] * ar[0] + ai[0] * ai[0]) + (ar[1] * ar[1] + ai[1] * ai[1])


def reader(own, others):
    half = own.shape[3] // 2

    def image(slot, tile):
        def value(part, parity):
            rows = pl.ds(parity, half, stride=2)
            if 0 <= slot < 2:
                return own[tile, slot, part, rows, :]
            here, there, turn = others[slot // 2]
            first = here[tile][slot % 2, part, rows, :]
            return first if there is None else jnp.where(turn, there[tile][slot % 2, part, rows, :], first)

        return [[value(part, parity) for parity in range(2)] for part in range(2)]

    return image


def fill(stage, image, tiles, half, pairs, slots):
    for tile in range(tiles):
        lanes = pl.ds(tile * LANES, LANES)
        loaded = {slot: image(slot, tile) for slot in {s for pair in pairs for s in pair} | set(slots)}
        values = [v for a, b in pairs for v in product(loaded[a], loaded[b])]
        values += [power(loaded[slot]) for slot in slots]
        for n, value in enumerate(values):
            stage[pl.ds(n * half, half), lanes] = value


def meet(stage, image, tiles, half, sent, side):
    fill(stage, image, tiles, half, SENT, (2, 3))
    at_left = lax.axis_index("col") == 0

    def border(slot):
        here, there = image(slot, tiles - 1), image(slot, 0)
        return [
            [jnp.where(at_left, pltpu.roll(v, STRIP, 1), w) for v, w in zip(p, q)]
            for p, q in zip(here, there)
        ]

    bordered = {slot: border(slot) for slot in range(-2, 4)}
    values = [v for a, b in CANDIDATES for v in product(bordered[a], bordered[b])]
    values += [power(bordered[slot]) for slot in range(-2, 4)]
    block = lane_index((half, LANES)) >> 5
    rows = pl.ds((2 * len(SENT) + 2) * half, half)
    for tile in range(tiles):
        row = jnp.zeros((half, LANES), F32)
        for k, value in enumerate(values[4 * tile : 4 * tile + 4]):
            row = jnp.where(block == k, pltpu.roll(value, STRIP * k, 1) if k else value, row)
        stage[rows, pl.ds(tile * LANES, LANES)] = row
    means = split_dot(stage[...], looks_table(tiles * LANES))
    end = (2 * len(SENT) + 2) * half
    sent[...] = means[:end]
    side[...] = means[end:]


def meet_kernel(*refs):
    own, (sent, side, stage) = refs[0], refs[-3:]
    tiles, half = own.shape[0], own.shape[3] // 2
    before, before_wrap, after = [refs[1 + n * tiles : 1 + (n + 1) * tiles] for n in range(3)]
    first = lax.axis_index("date") % RUN == 0
    image = reader(own, {-1: (before, before_wrap, first), 1: (after, None, None)})
    meet(stage, image, tiles, half, sent, side)


def held_kernel(*refs):
    own, (held, sent, side, stage, second) = refs[0], refs[-5:]
    tiles, half = own.shape[0], own.shape[3] // 2
    after, after_wrap, before = [refs[1 + n * tiles : 1 + (n + 1) * tiles] for n in range(3)]
    last = lax.axis_index("date") % RUN == RUN - 1
    fill(stage, reader(own, {1: (after, after_wrap, last)}), tiles, half, HELD, range(4))
    held[...] = split_dot(stage[...], looks_table(tiles * LANES))

    @pl.when(last)
    def _():
        image = reader(own, {-1: (before, None, None), 1: (after_wrap, None, None)})
        meet(second, image, tiles, half, sent, side)


def on_tiles(kernel, counts, stages, own, *images, behind=()):
    rows, cols = images[0].shape[2:]
    half = rows // 2
    whole = lambda shape: pl.BlockSpec(shape, lambda i: (0,) * len(shape))
    return pl.pallas_call(
        kernel,
        grid=(1,),
        out_shape=tuple(jax.ShapeDtypeStruct((count * half, LANES), F32) for count in counts),
        in_specs=[whole(own.shape)] + [spec for image in images for spec in tiled(image)]
        + [whole(value.shape) for value in behind],
        out_specs=tuple(whole((count * half, LANES)) for count in counts),
        scratch_shapes=[pltpu.VMEM((count * half, cols), F32) for count in stages],
        compiler_params=pltpu.CompilerParams(vmem_limit_bytes=32 * 1024 * 1024),
    )(own, *[image for image in images for _ in range(cols // LANES)], *behind)


def rims_kernel(secondaries, held, side, back, late_side, late_back, picked, chip, across, every):
    at_left = lax.axis_index("col") == 0
    lanes = lane_index((KEEP, LANES))
    place = jnp.where(at_left, RIGHT, 0)
    margin = (lanes >= place) & (lanes < place + MARGIN)
    late = lax.axis_index("date") % RUN == RUN - 2
    columns = jnp.where(late, late_side[...], side[...])
    held_at, back_at = 0, 0
    for n in range(PLANES):
        pair = n // 2
        from_back = pair in (3, 6, 7) or n >= PLANES - 2
        if from_back:
            rows = pl.ds(back_at * KEEP, KEEP)
            value, back_at = jnp.where(late, late_back[rows, :], back[rows, :]), back_at + 1
        else:
            value, held_at = held[pl.ds(held_at * KEEP, KEEP), :], held_at + 1
        here = MARGIN + MARGIN * n
        right = pltpu.roll(columns, (RIGHT - here) % LANES, 1)
        left = pltpu.roll(columns, -here % LANES, 1)
        every[pl.ds(n * KEEP, KEEP), :] = jnp.where(margin, jnp.where(at_left, right, left), value)

    first = 2 * lax.axis_index("date")
    dates = 2 * lax.axis_size("date")
    even = lax.axis_index("row") % 2 == 0
    starts = []
    for date in range(2):
        for link in range(LINKS):
            slot = (secondaries[date, link] - first + dates) % dates
            pair = 3 * date + slot - 1
            starts += [2 * pair, 2 * pair + 1, PLANES - 6 + slot]
    starts += [PLANES - 6 + date for date in range(2)]
    for n, start in enumerate(starts):
        at = start * KEEP if isinstance(start, int) else pl.multiple_of(start * KEEP, 8)
        value = every[pl.ds(at, KEEP), :]
        picked[pl.ds(n * KEEP, KEEP), :] = value
        top, bottom = value[:MARGIN], value[KEEP - MARGIN :]
        chip[pl.ds(MARGIN * n, MARGIN), :] = jnp.where(even, bottom, top)
        across[pl.ds(MARGIN * n, MARGIN), :] = jnp.where(even, top, bottom)


@functools.lru_cache(None)
def tables():
    blocks = LANES // PATCH
    n = np.arange(PATCH)
    angle = 2.0 * np.pi * (np.outer(n, n) % PATCH) / PATCH
    cosine, sine = np.cos(angle), np.sin(angle)
    forward = np.zeros((LANES, 2 * LANES))
    spread = np.zeros((LANES, 2 * LANES))
    inverse = np.zeros((LANES, 2 * LANES))
    for b in range(blocks):
        f = slice(b * PATCH, (b + 1) * PATCH)
        x = slice(b * KEEP, b * KEEP + PATCH)
        o = slice(b * KEEP, (b + 1) * KEEP)
        kept = slice(MARGIN, MARGIN + KEEP)
        forward[x, f] = cosine
        forward[x, LANES + b * PATCH : LANES + (b + 1) * PATCH] = -sine
        inverse[f, o] = cosine[:, kept] / PATCH
        inverse[f, LANES + b * KEEP : LANES + (b + 1) * KEEP] = sine[:, kept] / PATCH
        near = (n[:, None] - n[None, :]) % PATCH
        spread[f, f] = (near == 0) | (near == 1) | (near == PATCH - 1)
        spread[f, LANES + b * PATCH : LANES + (b + 1) * PATCH] = 1.0
    down = np.block([[cosine, sine], [-sine, cosine]])
    kept = slice(MARGIN, MARGIN + KEEP)
    up = np.block([[cosine[kept], -sine[kept]], [sine[kept], cosine[kept]]]) / PATCH
    return [np.asarray(t, np.float32) for t in (forward, spread, inverse, down, up)]


def exact_dot(a, b):
    return jnp.dot(a, b, preferred_element_type=F32, precision=lax.Precision.HIGHEST)


def filter_kernel(picked, across, chip, forward, spread, inverse, down, up, filtered, coherent, pad):
    even = lax.axis_index("row") % 2 == 0
    pairs = 2 * LINKS
    for n in range(3 * pairs + 2):
        near, far = chip[pl.ds(MARGIN * n, MARGIN), :], across[pl.ds(MARGIN * n, MARGIN), :]
        pad[n, pl.ds(0, MARGIN), :] = jnp.where(even, far, near)
        pad[n, pl.ds(MARGIN, KEEP), :] = picked[pl.ds(n * KEEP, KEEP), :]
        pad[n, pl.ds(MARGIN + KEEP, MARGIN), :] = jnp.where(even, near, far)

    def box(value):
        rows = value[3 : 3 + KEEP] + value[4 : 4 + KEEP] + value[5 : 5 + KEEP]
        total = pltpu.roll(rows, LANES - 3, 1) + pltpu.roll(rows, LANES - 4, 1) + pltpu.roll(rows, LANES - 5, 1)
        return total * (1.0 / 9.0)

    wide = coherent.shape[-1]
    firsts = [box(pad[3 * pairs + date]) for date in range(2)]
    for p in range(pairs):
        real, imag, second = [box(pad[3 * p + k]) for k in range(3)]
        factor = lax.rsqrt(firsts[p // LINKS] * second + 1e-06)
        coherent[p // LINKS, p % LINKS, 0] = (real * factor)[:, :wide]
        coherent[p // LINKS, p % LINKS, 1] = (imag * factor)[:, :wide]

    reals = jnp.concatenate([pad[3 * p] for p in range(pairs)], axis=0)
    imags = jnp.concatenate([pad[3 * p + 1] for p in range(pairs)], axis=0)
    size = pairs * PATCH
    across_cols = exact_dot(jnp.concatenate([reals, imags], axis=0), forward[...])
    col_real = across_cols[:size, :LANES] - across_cols[size:, LANES:]
    col_imag = across_cols[size:, :LANES] + across_cols[:size, LANES:]
    rows_of = lambda v, p, count: v[p * count : (p + 1) * count]
    stacked = jnp.concatenate(
        [
            jnp.concatenate([rows_of(col_real, p, PATCH), rows_of(col_imag, p, PATCH)], axis=0)
            for p in range(pairs)
        ],
        axis=1,
    )
    spectrum = exact_dot(down[...], stacked)
    real, imag = spectrum[:PATCH], spectrum[PATCH:]
    power = real * real + imag * imag
    lanes_of = lambda v, p: v[:, p * LANES : (p + 1) * LANES]
    tall = lambda v: jnp.concatenate([lanes_of(v, p) for p in range(pairs)], axis=0)
    sums = exact_dot(tall(power), spread[...])
    weights = []
    for p in range(pairs):
        near = rows_of(sums, p, PATCH)[:, :LANES]
        level = jnp.sum(rows_of(sums, p, PATCH)[:, LANES:], axis=0, keepdims=True) * (1.0 / (PATCH * PATCH))
        smooth = (near + pltpu.roll(near, 1, 0) + pltpu.roll(near, PATCH - 1, 0)) * (1.0 / 9.0)
        weights.append(jnp.sqrt(jnp.sqrt(smooth + level + 1e-06)))
    totals = exact_dot(jnp.concatenate(weights, axis=0), spread[:, LANES:])
    scaled = []
    for p in range(pairs):
        total = jnp.sum(rows_of(totals, p, PATCH), axis=0, keepdims=True)
        scaled.append(weights[p] * ((PATCH * PATCH) / total))
    weight = jnp.concatenate(scaled, axis=1)
    lifted = exact_dot(up[...], jnp.concatenate([real * weight, imag * weight], axis=0))
    low, high = lifted[:KEEP], lifted[KEEP:]
    size = pairs * KEEP
    result = exact_dot(jnp.concatenate([tall(low), tall(high)], axis=0), inverse[...])
    out_real = result[:size, :LANES] - result[size:, LANES:]
    out_imag = result[size:, :LANES] + result[:size, LANES:]
    for p in range(pairs):
        filtered[p // LINKS, p % LINKS, 0] = rows_of(out_real, p, KEEP)[:, :wide]
        filtered[p // LINKS, p % LINKS, 1] = rows_of(out_imag, p, KEEP)[:, :wide]


def body(images, secondaries):
    rows, cols = images.shape[2:]
    cells_down, cells_along = rows // 2, cols // 8
    dates, count = lax.axis_size("date"), lax.axis_size("row")
    inner = lambda steps: [(d, d + steps) for d in range(dates) if 0 <= d % RUN + steps < RUN]
    outer = lambda steps: [(d, (d + steps) % dates) for d in range(dates) if not 0 <= d % RUN + steps < RUN]
    along = lambda value, pairs: lax.ppermute(value, "date", pairs)
    across = lambda value, pairs: lax.ppermute(
        value, ("date", "col"), [(2 * d + c, 2 * e + (c ^ 1)) for d, e in pairs for c in range(2)]
    )
    after, before = along(images, inner(-1)), along(images, inner(1))
    after_wrap, before_wrap = along(images, outer(-1)), along(images, outer(1))
    own = kept(images)
    total = 2 * len(SENT) + 2
    sent, side = on_tiles(meet_kernel, (total, 1), (total + 1,), own, before, before_wrap, after)
    soon = [(d, (d - 1) % dates) for d in range(dates) if d % RUN < RUN - 1]
    late = [(d, d - 1) for d in range(dates) if d % RUN == RUN - 1]
    side, back = across(side, soon), along(sent, soon)
    keeps = 2 * len(HELD) + 4
    held, late_sent, late_side = on_tiles(
        held_kernel, (keeps, total, 1), (keeps, total + 1), own, after, after_wrap, before, behind=(side, back)
    )
    late_side, late_back = across(late_side, late), along(late_sent, late)

    planes = 3 * 2 * LINKS + 2
    rim = jax.ShapeDtypeStruct((planes * MARGIN, LANES), F32)
    every = pltpu.VMEM((PLANES * cells_down, LANES), F32)
    picked = jax.ShapeDtypeStruct((planes * cells_down, LANES), F32)
    picked, chip, across = call(rims_kernel, (picked, rim, rim), 6, [every], [smem()] + [vmem()] * 5)(
        secondaries, held, side, back, late_side, late_back
    )
    chip = lax.ppermute(chip, "row", [(i, i ^ 1) for i in range(count)])
    across = lax.ppermute(across, "row", [(i, ((i + 1) ^ 1) - 1) for i in range(1, count - 1)])
    out = jax.ShapeDtypeStruct((2, LINKS, 2, cells_down, cells_along), F32)
    return call(filter_kernel, (out, out), 8, [pltpu.VMEM((planes, PATCH, LANES), F32)])(
        picked, across, chip, *tables()
    )


def solution(mesh):
    in_specs = (P("date", None, "row", "col"), P("date", None))
    out_specs = (P("date", None, None, "row", "col"), P("date", None, None, "row", "col"))
    return jax.shard_map(body, mesh=mesh, in_specs=in_specs, out_specs=out_specs, check_vma=False)
```

```python
import functools
import math

import jax
import jax.numpy as jnp
import numpy as np
from jax import lax
from jax.experimental import pallas as pl
from jax.experimental.pallas import tpu as pltpu
from jax.sharding import PartitionSpec as P

KEEP = 24
PATCH = 32
MARGIN = 4
LANES = 128
STRIP = 32
RIGHT = 100
LINKS = 3
RUN = 16
F32 = jnp.float32
BF16 = jnp.bfloat16

HELD = ((0, 1), (0, 2), (0, 3), (1, 2), (1, 3))
SENT = ((-2, 2), (-1, 2), (-1, 3))
CANDIDATES = tuple((a - 2, b - 2) for a in range(2) for b in range(a + 1, a + 5))
PLANES = 2 * len(CANDIDATES) + 6


def vmem():
    return pl.BlockSpec(memory_space=pltpu.VMEM)


def smem():
    return pl.BlockSpec(memory_space=pltpu.SMEM)


def call(kernel, outs, count, scratch=(), specs=None, flops=1e6, moved=1e6):
    return pl.pallas_call(
        kernel,
        out_shape=outs,
        in_specs=specs or [vmem()] * count,
        out_specs=jax.tree.map(lambda _: vmem(), outs),
        scratch_shapes=list(scratch),
        compiler_params=pltpu.CompilerParams(vmem_limit_bytes=32 * 1024 * 1024),
        cost_estimate=pl.CostEstimate(flops=int(flops), bytes_accessed=int(moved), transcendentals=0),
    )


def lane_index(shape):
    return lax.broadcasted_iota(jnp.int32, shape, len(shape) - 1)


def looks_table(cols):
    source = lax.broadcasted_iota(jnp.int32, (cols, LANES), 0)
    target = lax.broadcasted_iota(jnp.int32, (cols, LANES), 1)
    return jnp.where((source >> 3) + MARGIN == target, 1.0 / 16.0, 0.0).astype(BF16)


def split_dot(values, table):
    high = values.astype(BF16)
    rest = values - high.astype(F32)
    middle = rest.astype(BF16)
    low = (rest - middle.astype(F32)).astype(BF16)
    dot = lambda v: jnp.dot(v, table, preferred_element_type=F32)
    return dot(high) + (dot(middle) + dot(low))


def tiled(images):
    rows, cols = images.shape[2:]
    spec = lambda index: pl.BlockSpec((2, 2, rows, LANES), lambda i: (0, 0, 0, index))
    return [spec(index) for index in range(cols // LANES)]


def keep_kernel(secondaries, source, target, slots, arrived):
    copies = [
        pltpu.make_async_copy(
            source.at[:, :, :, pl.ds(tile * LANES, LANES)], target.at[tile], arrived.at[tile]
        )
        for tile in range(target.shape[0])
    ]
    for copy in copies:
        copy.start()
    first = 2 * lax.axis_index("date")
    dates = 2 * lax.axis_size("date")
    for date in range(2):
        for link in range(LINKS):
            slot = (secondaries[date, link] - first + dates) % dates
            slots[pl.ds(LINKS * date + link, 1), :] = jnp.full((1, LANES), slot, jnp.int32)
    for copy in copies:
        copy.wait()


def kept(images, secondaries):
    tiles = images.shape[3] // LANES
    return pl.pallas_call(
        keep_kernel,
        out_shape=(
            pltpu.VMEM((tiles,) + images.shape[:3] + (LANES,), F32),
            pltpu.VMEM((8, LANES), jnp.int32),
        ),
        in_specs=[smem(), pl.BlockSpec(memory_space=pl.ANY)],
        out_specs=(vmem(), vmem()),
        scratch_shapes=[pltpu.SemaphoreType.DMA((tiles,))],
    )(secondaries, images)


def product(a, b):
    (ar, ai), (br, bi) = a, b
    real = (ar[0] * br[0] + ai[0] * bi[0]) + (ar[1] * br[1] + ai[1] * bi[1])
    imag = (ai[0] * br[0] - ar[0] * bi[0]) + (ai[1] * br[1] - ar[1] * bi[1])
    return real, imag


def power(a):
    ar, ai = a
    return (ar[0] * ar[0] + ai[0] * ai[0]) + (ar[1] * ar[1] + ai[1] * ai[1])


def reader(own, others):
    half = own.shape[3] // 2

    def image(slot, tile):
        def value(part, parity):
            rows = pl.ds(parity, half, stride=2)
            if 0 <= slot < 2:
                return own[tile, slot, part, rows, :]
            here, there, turn = others[slot // 2]
            first = here[tile][slot % 2, part, rows, :]
            return first if there is None else jnp.where(turn, there[tile][slot % 2, part, rows, :], first)

        return [[value(part, parity) for parity in range(2)] for part in range(2)]

    return image


def fill(stage, image, tiles, half, pairs, slots):
    for tile in range(tiles):
        lanes = pl.ds(tile * LANES, LANES)
        loaded = {slot: image(slot, tile) for slot in {s for pair in pairs for s in pair} | set(slots)}
        values = [v for a, b in pairs for v in product(loaded[a], loaded[b])]
        values += [power(loaded[slot]) for slot in slots]
        for n, value in enumerate(values):
            stage[pl.ds(n * half, half), lanes] = value


def meet(stage, image, tiles, half, wanted, *outs):
    pairs, slots = wanted
    fill(stage, image, tiles, half, pairs, slots)
    at_left = lax.axis_index("col") == 0

    def border(slot):
        here, there = image(slot, tiles - 1), image(slot, 0)
        return [
            [jnp.where(at_left, pltpu.roll(v, STRIP, 1), w) for v, w in zip(p, q)]
            for p, q in zip(here, there)
        ]

    bordered = {slot: border(slot) for slot in range(-2, 4)}
    values = [v for a, b in CANDIDATES for v in product(bordered[a], bordered[b])]
    values += [power(bordered[slot]) for slot in range(-2, 4)]
    block = lane_index((half, LANES)) >> 5
    rows = pl.ds((2 * len(pairs) + len(slots)) * half, half)
    for tile in range(tiles):
        row = jnp.zeros((half, LANES), F32)
        for k, value in enumerate(values[4 * tile : 4 * tile + 4]):
            row = jnp.where(block == k, pltpu.roll(value, STRIP * k, 1) if k else value, row)
        stage[rows, pl.ds(tile * LANES, LANES)] = row
    means = split_dot(stage[...], looks_table(tiles * LANES))
    at = 0
    for out in outs:
        out[...] = means[at : at + out.shape[0]]
        at += out.shape[0]


ALL = (HELD + SENT, (0, 1, 2, 3))
GOING = (SENT, (2, 3))


def near_kernel(*refs):
    own, (held, sent, side, stage, means) = refs[0], refs[-5:]
    tiles, half = own.shape[0], own.shape[3] // 2
    after, before = [refs[1 + n * tiles : 1 + (n + 1) * tiles] for n in range(2)]

    @pl.when(lax.axis_index("date") % RUN < RUN - 1)
    def _():
        image = reader(own, {-1: (before, None, None), 1: (after, None, None)})
        meet(stage, image, tiles, half, ALL, means, side)
        share(means, half, held, sent)


def share(means, half, held, sent):
    kept, going = 2 * len(HELD) * half, 2 * len(SENT) * half
    held[pl.ds(0, kept), :] = means[pl.ds(0, kept), :]
    held[pl.ds(kept, 4 * half), :] = means[pl.ds(kept + going, 4 * half), :]
    sent[pl.ds(0, going), :] = means[pl.ds(kept, going), :]
    sent[pl.ds(going, 2 * half), :] = means[pl.ds(kept + going + 2 * half, 2 * half), :]


def end_kernel(run, own, before, after, *refs):
    count = 2 if run == 0 else 4
    outs, (stage, mine, near, arrived) = refs[-4 - count : -4], refs[-4:]
    tiles, half = own.shape[0], own.shape[3] // 2

    @pl.when(lax.axis_index("date") % RUN == run)
    def _():
        copies = [pltpu.make_async_copy(own, mine, arrived.at[0, 0])]
        for n, source in enumerate((before, after)):
            for tile in range(tiles):
                lanes = pl.ds(tile * LANES, LANES)
                copies.append(
                    pltpu.make_async_copy(source.at[:, :, :, lanes], near.at[n, tile], arrived.at[n + 1, tile])
                )
        for copy in copies:
            copy.start()
        for copy in copies:
            copy.wait()
        blocks = [[near.at[n, tile] for tile in range(tiles)] for n in range(2)]
        image = reader(mine, {-1: (blocks[0], None, None), 1: (blocks[1], None, None)})
        if run == 0:
            meet(stage, image, tiles, half, GOING, *outs)
        else:
            held, sent, side, means = outs
            meet(stage, image, tiles, half, ALL, means, side)
            share(means, half, held, sent)


def planes_of(rows, *counts):
    return tuple(jax.ShapeDtypeStruct((count * rows // 2, LANES), F32) for count in counts)


STAYING, LEAVING = 2 * len(HELD) + 4, 2 * len(SENT) + 2
BOTH = 2 * len(HELD + SENT) + 4


def at_end(run, own, before, after, *behind):
    rows, cols = after.shape[2:]
    half, tiles = rows // 2, cols // LANES
    outs = (LEAVING, 1) if run == 0 else (STAYING, LEAVING, 1)
    total = LEAVING if run == 0 else BOTH
    scratch = [
        pltpu.VMEM(((total + 1) * half, cols), F32),
        pltpu.VMEM(own.shape, F32),
        pltpu.VMEM((2,) + own.shape, F32),
        pltpu.SemaphoreType.DMA((3, tiles)),
    ]
    return call(
        functools.partial(end_kernel, run),
        planes_of(rows, *outs),
        3 + len(behind),
        ([] if run == 0 else [pltpu.VMEM((BOTH * half, LANES), F32)]) + scratch,
        [pl.BlockSpec(memory_space=pl.ANY)] * (3 + len(behind)),
    )(own, before, after, *behind)


def near(own, *images):
    rows, cols = images[0].shape[2:]
    half = rows // 2
    whole = lambda shape: pl.BlockSpec(shape, lambda i: (0,) * len(shape))
    outs = planes_of(rows, STAYING, LEAVING, 1)
    return pl.pallas_call(
        near_kernel,
        grid=(1,),
        out_shape=outs,
        in_specs=[whole(own.shape)] + [spec for image in images for spec in tiled(image)],
        out_specs=tuple(whole(out.shape) for out in outs),
        scratch_shapes=[pltpu.VMEM(((BOTH + 1) * half, cols), F32), pltpu.VMEM((BOTH * half, LANES), F32)],
        compiler_params=pltpu.CompilerParams(vmem_limit_bytes=32 * 1024 * 1024),
    )(own, *[image for image in images for _ in range(cols // LANES)])


def rims_kernel(
    slots,
    held,
    last_held,
    side,
    back,
    low_side,
    low_back,
    high_side,
    high_back,
    picked,
    chip,
    across,
    every,
):
    at_left = lax.axis_index("col") == 0
    lanes = lane_index((KEEP, LANES))
    edge = jnp.where(at_left, RIGHT, 0)
    margin = (lanes >= edge) & (lanes < edge + MARGIN)
    place = lax.axis_index("date") % RUN
    from_low, from_high = place == RUN - 1, place == RUN - 2
    columns = jnp.where(from_low, low_side[...], jnp.where(from_high, high_side[...], side[...]))
    held_at, back_at = 0, 0
    for n in range(PLANES):
        pair = n // 2
        from_back = pair in (3, 6, 7) or n >= PLANES - 2
        if from_back:
            rows = pl.ds(back_at * KEEP, KEEP)
            value = jnp.where(from_high, high_back[rows, :], back[rows, :])
            value, back_at = jnp.where(from_low, low_back[rows, :], value), back_at + 1
        else:
            rows = pl.ds(held_at * KEEP, KEEP)
            value, held_at = jnp.where(from_low, last_held[rows, :], held[rows, :]), held_at + 1
        here = MARGIN + MARGIN * n
        right = pltpu.roll(columns, (RIGHT - here) % LANES, 1)
        left = pltpu.roll(columns, -here % LANES, 1)
        every[pl.ds(n * KEEP, KEEP), :] = jnp.where(margin, jnp.where(at_left, right, left), value)

    even = lax.axis_index("row") % 2 == 0
    plane = lambda n: every[pl.ds(n * KEEP, KEEP), :]
    chosen = []
    for date in range(2):
        for link in range(LINKS):
            slot = jnp.broadcast_to(slots[pl.ds(LINKS * date + link, 1), :], (KEEP, LANES))
            triples = [
                (plane(2 * (3 * date + n - 1)), plane(2 * (3 * date + n - 1) + 1), plane(PLANES - 6 + n))
                for n in range(date + 1, date + 5)
            ]
            values = triples[0]
            for n, triple in zip(range(date + 2, date + 5), triples[1:]):
                values = [jnp.where(slot == n, v, w) for v, w in zip(triple, values)]
            chosen += values
    chosen += [plane(PLANES - 6 + date) for date in range(2)]
    for n, value in enumerate(chosen):
        picked[pl.ds(n * KEEP, KEEP), :] = value
        top, bottom = value[:MARGIN], value[KEEP - MARGIN :]
        chip[pl.ds(MARGIN * n, MARGIN), :] = jnp.where(even, bottom, top)
        across[pl.ds(MARGIN * n, MARGIN), :] = jnp.where(even, top, bottom)


@functools.lru_cache(None)
def tables():
    blocks = LANES // PATCH
    n = np.arange(PATCH)
    angle = 2.0 * np.pi * (np.outer(n, n) % PATCH) / PATCH
    cosine, sine = np.cos(angle), np.sin(angle)
    forward = np.zeros((LANES, 2 * LANES))
    spread = np.zeros((LANES, 2 * LANES))
    inverse = np.zeros((LANES, 2 * LANES))
    for b in range(blocks):
        f = slice(b * PATCH, (b + 1) * PATCH)
        x = slice(b * KEEP, b * KEEP + PATCH)
        o = slice(b * KEEP, (b + 1) * KEEP)
        kept = slice(MARGIN, MARGIN + KEEP)
        forward[x, f] = cosine
        forward[x, LANES + b * PATCH : LANES + (b + 1) * PATCH] = -sine
        inverse[f, o] = cosine[:, kept] / PATCH
        inverse[f, LANES + b * KEEP : LANES + (b + 1) * KEEP] = sine[:, kept] / PATCH
        near = (n[:, None] - n[None, :]) % PATCH
        spread[f, f] = (near == 0) | (near == 1) | (near == PATCH - 1)
        spread[f, LANES + b * PATCH : LANES + (b + 1) * PATCH] = 1.0
    down = np.block([[cosine, sine], [-sine, cosine]])
    kept = slice(MARGIN, MARGIN + KEEP)
    up = np.block([[cosine[kept], -sine[kept]], [sine[kept], cosine[kept]]]) / PATCH
    return [np.asarray(t, np.float32) for t in (forward, spread, inverse, down, up)]


def exact_dot(a, b):
    return jnp.dot(a, b, preferred_element_type=F32, precision=lax.Precision.HIGHEST)


def filter_kernel(picked, across, chip, forward, spread, inverse, down, up, filtered, coherent, pad):
    even = lax.axis_index("row") % 2 == 0
    pairs = 2 * LINKS
    for n in range(3 * pairs + 2):
        near, far = chip[pl.ds(MARGIN * n, MARGIN), :], across[pl.ds(MARGIN * n, MARGIN), :]
        pad[n, pl.ds(0, MARGIN), :] = jnp.where(even, far, near)
        pad[n, pl.ds(MARGIN, KEEP), :] = picked[pl.ds(n * KEEP, KEEP), :]
        pad[n, pl.ds(MARGIN + KEEP, MARGIN), :] = jnp.where(even, near, far)

    def box(value):
        rows = value[3 : 3 + KEEP] + value[4 : 4 + KEEP] + value[5 : 5 + KEEP]
        total = pltpu.roll(rows, LANES - 3, 1) + pltpu.roll(rows, LANES - 4, 1) + pltpu.roll(rows, LANES - 5, 1)
        return total * (1.0 / 9.0)

    wide = coherent.shape[-1]
    firsts = [box(pad[3 * pairs + date]) for date in range(2)]
    for p in range(pairs):
        real, imag, second = [box(pad[3 * p + k]) for k in range(3)]
        factor = lax.rsqrt(firsts[p // LINKS] * second + 1e-06)
        coherent[p // LINKS, p % LINKS, 0] = (real * factor)[:, :wide]
        coherent[p // LINKS, p % LINKS, 1] = (imag * factor)[:, :wide]

    reals = jnp.concatenate([pad[3 * p] for p in range(pairs)], axis=0)
    imags = jnp.concatenate([pad[3 * p + 1] for p in range(pairs)], axis=0)
    size = pairs * PATCH
    across_cols = exact_dot(jnp.concatenate([reals, imags], axis=0), forward[...])
    col_real = across_cols[:size, :LANES] - across_cols[size:, LANES:]
    col_imag = across_cols[size:, :LANES] + across_cols[:size, LANES:]
    rows_of = lambda v, p, count: v[p * count : (p + 1) * count]
    stacked = jnp.concatenate(
        [
            jnp.concatenate([rows_of(col_real, p, PATCH), rows_of(col_imag, p, PATCH)], axis=0)
            for p in range(pairs)
        ],
        axis=1,
    )
    spectrum = exact_dot(down[...], stacked)
    real, imag = spectrum[:PATCH], spectrum[PATCH:]
    power = real * real + imag * imag
    lanes_of = lambda v, p: v[:, p * LANES : (p + 1) * LANES]
    tall = lambda v: jnp.concatenate([lanes_of(v, p) for p in range(pairs)], axis=0)
    sums = exact_dot(tall(power), spread[...])
    weights = []
    for p in range(pairs):
        near = rows_of(sums, p, PATCH)[:, :LANES]
        level = jnp.sum(rows_of(sums, p, PATCH)[:, LANES:], axis=0, keepdims=True) * (1.0 / (PATCH * PATCH))
        smooth = (near + pltpu.roll(near, 1, 0) + pltpu.roll(near, PATCH - 1, 0)) * (1.0 / 9.0)
        weights.append(jnp.sqrt(jnp.sqrt(smooth + level + 1e-06)))
    totals = exact_dot(jnp.concatenate(weights, axis=0), spread[:, LANES:])
    scaled = []
    for p in range(pairs):
        total = jnp.sum(rows_of(totals, p, PATCH), axis=0, keepdims=True)
        scaled.append(weights[p] * ((PATCH * PATCH) / total))
    weight = jnp.concatenate(scaled, axis=1)
    lifted = exact_dot(up[...], jnp.concatenate([real * weight, imag * weight], axis=0))
    low, high = lifted[:KEEP], lifted[KEEP:]
    size = pairs * KEEP
    result = exact_dot(jnp.concatenate([tall(low), tall(high)], axis=0), inverse[...])
    out_real = result[:size, :LANES] - result[size:, LANES:]
    out_imag = result[size:, :LANES] + result[:size, LANES:]
    for p in range(pairs):
        filtered[p // LINKS, p % LINKS, 0] = rows_of(out_real, p, KEEP)[:, :wide]
        filtered[p // LINKS, p % LINKS, 1] = rows_of(out_imag, p, KEEP)[:, :wide]


def body(images, secondaries):
    rows, cols = images.shape[2:]
    cells_down, cells_along = rows // 2, cols // 8
    dates, count = lax.axis_size("date"), lax.axis_size("row")
    inner = lambda steps: [(d, d + steps) for d in range(dates) if 0 <= d % RUN + steps < RUN]
    outer = lambda steps: [(d, (d + steps) % dates) for d in range(dates) if not 0 <= d % RUN + steps < RUN]
    along = lambda value, pairs: lax.ppermute(value, "date", pairs)
    across = lambda value, pairs: lax.ppermute(
        value, ("date", "col"), [(2 * d + c, 2 * e + (c ^ 1)) for d, e in pairs for c in range(2)]
    )
    after, before = along(images, inner(-1)), along(images, inner(1))
    after_wrap, before_wrap = along(images, outer(-1)), along(images, outer(1))
    own, slots = kept(images, secondaries)
    step = lambda wanted: [(d, (d - 1) % dates) for d in range(dates) if wanted(d % RUN)]
    middle, low, high = step(lambda n: 0 < n < RUN - 1), step(lambda n: n == 0), step(lambda n: n == RUN - 1)
    held, sent, side = near(own, after, before)
    side, back = across(side, middle), along(sent, middle)
    sent, low_side = at_end(0, own, before_wrap, after, side, back, before)
    low_side, low_back = across(low_side, low), along(sent, low)
    last_held, sent, high_side = at_end(RUN - 1, own, before, after_wrap, low_side, low_back)
    high_side, high_back = across(high_side, high), along(sent, high)

    planes = 3 * 2 * LINKS + 2
    rim = jax.ShapeDtypeStruct((planes * MARGIN, LANES), F32)
    every = pltpu.VMEM((PLANES * cells_down, LANES), F32)
    picked = jax.ShapeDtypeStruct((planes * cells_down, LANES), F32)
    picked, chip, across = call(rims_kernel, (picked, rim, rim), 9, [every])(
        slots, held, last_held, side, back, low_side, low_back, high_side, high_back
    )
    chip = lax.ppermute(chip, "row", [(i, i ^ 1) for i in range(count)])
    across = lax.ppermute(across, "row", [(i, ((i + 1) ^ 1) - 1) for i in range(1, count - 1)])
    out = jax.ShapeDtypeStruct((2, LINKS, 2, cells_down, cells_along), F32)
    return call(filter_kernel, (out, out), 8, [pltpu.VMEM((planes, PATCH, LANES), F32)])(
        picked, across, chip, *tables()
    )


def solution(mesh):
    in_specs = (P("date", None, "row", "col"), P("date", None))
    out_specs = (P("date", None, None, "row", "col"), P("date", None, None, "row", "col"))
    return jax.shard_map(body, mesh=mesh, in_specs=in_specs, out_specs=out_specs, check_vma=False)
```

```python
import functools
import math

import jax
import jax.numpy as jnp
import numpy as np
from jax import lax
from jax.experimental import pallas as pl
from jax.experimental.pallas import tpu as pltpu
from jax.sharding import PartitionSpec as P

KEEP = 24
PATCH = 32
MARGIN = 4
LANES = 128
STRIP = 32
RIGHT = 100
LINKS = 3
RUN = 16
F32 = jnp.float32
BF16 = jnp.bfloat16

HELD = ((0, 1), (0, 2), (0, 3), (1, 2), (1, 3))
SENT = ((-2, 2), (-1, 2), (-1, 3))
CANDIDATES = tuple((a - 2, b - 2) for a in range(2) for b in range(a + 1, a + 5))
PLANES = 2 * len(CANDIDATES) + 6


def vmem():
    return pl.BlockSpec(memory_space=pltpu.VMEM)


def smem():
    return pl.BlockSpec(memory_space=pltpu.SMEM)


def call(kernel, outs, count, scratch=(), specs=None, flops=1e6, moved=1e6):
    return pl.pallas_call(
        kernel,
        out_shape=outs,
        in_specs=specs or [vmem()] * count,
        out_specs=jax.tree.map(lambda _: vmem(), outs),
        scratch_shapes=list(scratch),
        compiler_params=pltpu.CompilerParams(vmem_limit_bytes=32 * 1024 * 1024),
        cost_estimate=pl.CostEstimate(flops=int(flops), bytes_accessed=int(moved), transcendentals=0),
    )


def lane_index(shape):
    return lax.broadcasted_iota(jnp.int32, shape, len(shape) - 1)


def looks_table(cols):
    source = lax.broadcasted_iota(jnp.int32, (cols, LANES), 0)
    target = lax.broadcasted_iota(jnp.int32, (cols, LANES), 1)
    return jnp.where((source >> 3) + MARGIN == target, 1.0 / 16.0, 0.0).astype(BF16)


def split_dot(values, table):
    high = values.astype(BF16)
    rest = values - high.astype(F32)
    middle = rest.astype(BF16)
    low = (rest - middle.astype(F32)).astype(BF16)
    dot = lambda v: jnp.dot(v, table, preferred_element_type=F32)
    return dot(high) + (dot(middle) + dot(low))


def tiled(images):
    rows, cols = images.shape[2:]
    spec = lambda index: pl.BlockSpec((2, 2, rows, LANES), lambda i: (0, 0, 0, index))
    return [spec(index) for index in range(cols // LANES)]


def keep_kernel(secondaries, source, target, slots, arrived):
    copies = [
        pltpu.make_async_copy(
            source.at[:, :, :, pl.ds(tile * LANES, LANES)], target.at[tile], arrived.at[tile]
        )
        for tile in range(target.shape[0])
    ]
    for copy in copies:
        copy.start()
    first = 2 * lax.axis_index("date")
    dates = 2 * lax.axis_size("date")
    for date in range(2):
        for link in range(LINKS):
            slot = (secondaries[date, link] - first + dates) % dates
            slots[pl.ds(LINKS * date + link, 1), :] = jnp.full((1, LANES), slot, jnp.int32)
    for copy in copies:
        copy.wait()


def kept(images, secondaries):
    tiles = images.shape[3] // LANES
    return pl.pallas_call(
        keep_kernel,
        out_shape=(
            pltpu.VMEM((tiles,) + images.shape[:3] + (LANES,), F32),
            pltpu.VMEM((8, LANES), jnp.int32),
        ),
        in_specs=[smem(), pl.BlockSpec(memory_space=pl.ANY)],
        out_specs=(vmem(), vmem()),
        scratch_shapes=[pltpu.SemaphoreType.DMA((tiles,))],
    )(secondaries, images)


def product(a, b):
    (ar, ai), (br, bi) = a, b
    real = (ar[0] * br[0] + ai[0] * bi[0]) + (ar[1] * br[1] + ai[1] * bi[1])
    imag = (ai[0] * br[0] - ar[0] * bi[0]) + (ai[1] * br[1] - ar[1] * bi[1])
    return real, imag


def power(a):
    ar, ai = a
    return (ar[0] * ar[0] + ai[0] * ai[0]) + (ar[1] * ar[1] + ai[1] * ai[1])


def reader(own, others):
    half = own.shape[3] // 2

    def image(slot, tile):
        def value(part, parity):
            rows = pl.ds(parity, half, stride=2)
            if 0 <= slot < 2:
                return own[tile, slot, part, rows, :]
            here, there, turn = others[slot // 2]
            first = here[tile][slot % 2, part, rows, :]
            return first if there is None else jnp.where(turn, there[tile][slot % 2, part, rows, :], first)

        return [[value(part, parity) for parity in range(2)] for part in range(2)]

    return image


def fill(stage, image, tiles, half, pairs, slots):
    for tile in range(tiles):
        lanes = pl.ds(tile * LANES, LANES)
        loaded = {slot: image(slot, tile) for slot in {s for pair in pairs for s in pair} | set(slots)}
        values = [v for a, b in pairs for v in product(loaded[a], loaded[b])]
        values += [power(loaded[slot]) for slot in slots]
        for n, value in enumerate(values):
            stage[pl.ds(n * half, half), lanes] = value


def meet(stage, image, tiles, half, wanted, *outs):
    pairs, slots = wanted
    fill(stage, image, tiles, half, pairs, slots)
    at_left = lax.axis_index("col") == 0

    def border(slot):
        here, there = image(slot, tiles - 1), image(slot, 0)
        return [
            [jnp.where(at_left, pltpu.roll(v, STRIP, 1), w) for v, w in zip(p, q)]
            for p, q in zip(here, there)
        ]

    bordered = {slot: border(slot) for slot in range(-2, 4)}
    values = [v for a, b in CANDIDATES for v in product(bordered[a], bordered[b])]
    values += [power(bordered[slot]) for slot in range(-2, 4)]
    block = lane_index((half, LANES)) >> 5
    rows = pl.ds((2 * len(pairs) + len(slots)) * half, half)
    for tile in range(tiles):
        row = jnp.zeros((half, LANES), F32)
        for k, value in enumerate(values[4 * tile : 4 * tile + 4]):
            row = jnp.where(block == k, pltpu.roll(value, STRIP * k, 1) if k else value, row)
        stage[rows, pl.ds(tile * LANES, LANES)] = row
    means = split_dot(stage[...], looks_table(tiles * LANES))
    at = 0
    for out in outs:
        out[...] = means[at : at + out.shape[0]]
        at += out.shape[0]


ALL = (HELD + SENT, (0, 1, 2, 3))
GOING = (SENT, (2, 3))


def near_kernel(*refs):
    own, (held, sent, side, stage, means) = refs[0], refs[-5:]
    tiles, half = own.shape[0], own.shape[3] // 2
    after, before = [refs[1 + n * tiles : 1 + (n + 1) * tiles] for n in range(2)]

    @pl.when(lax.axis_index("date") % RUN < RUN - 1)
    def _():
        image = reader(own, {-1: (before, None, None), 1: (after, None, None)})
        meet(stage, image, tiles, half, ALL, means, side)
        share(means, half, held, sent)


def share(means, half, held, sent):
    kept, going = 2 * len(HELD) * half, 2 * len(SENT) * half
    held[pl.ds(0, kept), :] = means[pl.ds(0, kept), :]
    held[pl.ds(kept, 4 * half), :] = means[pl.ds(kept + going, 4 * half), :]
    sent[pl.ds(0, going), :] = means[pl.ds(kept, going), :]
    sent[pl.ds(going, 2 * half), :] = means[pl.ds(kept + going + 2 * half, 2 * half), :]


def end_kernel(run, own, before, after, *refs):
    count = 2 if run == 0 else 4
    outs, (stage, mine, near, arrived) = refs[-4 - count : -4], refs[-4:]
    tiles, half = own.shape[0], own.shape[3] // 2

    @pl.when(lax.axis_index("date") % RUN == run)
    def _():
        copies = [pltpu.make_async_copy(own, mine, arrived.at[0, 0])]
        for n, source in enumerate((before, after)):
            for tile in range(tiles):
                lanes = pl.ds(tile * LANES, LANES)
                copies.append(
                    pltpu.make_async_copy(source.at[:, :, :, lanes], near.at[n, tile], arrived.at[n + 1, tile])
                )
        for copy in copies:
            copy.start()
        for copy in copies:
            copy.wait()
        blocks = [[near.at[n, tile] for tile in range(tiles)] for n in range(2)]
        image = reader(mine, {-1: (blocks[0], None, None), 1: (blocks[1], None, None)})
        if run == 0:
            sent, side = outs
            side[pl.ds(half, side.shape[0] - half), :] = jnp.zeros((side.shape[0] - half, LANES), F32)
            meet(stage, image, tiles, half, GOING, sent, side.at[pl.ds(0, half), :])
        else:
            held, sent, side, means = outs
            meet(stage, image, tiles, half, ALL, means, side)
            share(means, half, held, sent)


def planes_of(rows, *counts):
    return tuple(jax.ShapeDtypeStruct((count * rows // 2, LANES), F32) for count in counts)


STAYING, LEAVING = 2 * len(HELD) + 4, 2 * len(SENT) + 2
BOTH = 2 * len(HELD + SENT) + 4


def at_end(run, own, before, after, *behind):
    rows, cols = after.shape[2:]
    half, tiles = rows // 2, cols // LANES
    outs = (LEAVING, 8) if run == 0 else (STAYING, LEAVING, 1)
    total = LEAVING if run == 0 else BOTH
    scratch = [
        pltpu.VMEM(((total + 1) * half, cols), F32),
        pltpu.VMEM(own.shape, F32),
        pltpu.VMEM((2,) + own.shape, F32),
        pltpu.SemaphoreType.DMA((3, tiles)),
    ]
    return call(
        functools.partial(end_kernel, run),
        planes_of(rows, *outs),
        3 + len(behind),
        ([] if run == 0 else [pltpu.VMEM((BOTH * half, LANES), F32)]) + scratch,
        [pl.BlockSpec(memory_space=pl.ANY)] * (3 + len(behind)),
    )(own, before, after, *behind)


def near(own, *images):
    rows, cols = images[0].shape[2:]
    half = rows // 2
    whole = lambda shape: pl.BlockSpec(shape, lambda i: (0,) * len(shape))
    outs = planes_of(rows, STAYING, LEAVING, 1)
    return pl.pallas_call(
        near_kernel,
        grid=(1,),
        out_shape=outs,
        in_specs=[whole(own.shape)] + [spec for image in images for spec in tiled(image)],
        out_specs=tuple(whole(out.shape) for out in outs),
        scratch_shapes=[pltpu.VMEM(((BOTH + 1) * half, cols), F32), pltpu.VMEM((BOTH * half, LANES), F32)],
        compiler_params=pltpu.CompilerParams(vmem_limit_bytes=32 * 1024 * 1024),
    )(own, *[image for image in images for _ in range(cols // LANES)])


def merge_kernel(side, back, low_side, low_back, new_side, new_back):
    from_low = lax.axis_index("date") % RUN == RUN - 1
    new_side[...] = jnp.where(from_low, low_side[pl.ds(0, side.shape[0]), :], side[...])
    new_back[...] = jnp.where(from_low, low_back[...], back[...])


def rims_kernel(
    slots,
    held,
    last_held,
    side,
    back,
    high_side,
    high_back,
    picked,
    chip,
    across,
    every,
):
    at_left = lax.axis_index("col") == 0
    lanes = lane_index((KEEP, LANES))
    edge = jnp.where(at_left, RIGHT, 0)
    margin = (lanes >= edge) & (lanes < edge + MARGIN)
    place = lax.axis_index("date") % RUN
    from_low, from_high = place == RUN - 1, place == RUN - 2
    columns = jnp.where(from_high, high_side[...], side[...])
    held_at, back_at = 0, 0
    for n in range(PLANES):
        pair = n // 2
        from_back = pair in (3, 6, 7) or n >= PLANES - 2
        if from_back:
            rows = pl.ds(back_at * KEEP, KEEP)
            value, back_at = jnp.where(from_high, high_back[rows, :], back[rows, :]), back_at + 1
        else:
            rows = pl.ds(held_at * KEEP, KEEP)
            value, held_at = jnp.where(from_low, last_held[rows, :], held[rows, :]), held_at + 1
        here = MARGIN + MARGIN * n
        right = pltpu.roll(columns, (RIGHT - here) % LANES, 1)
        left = pltpu.roll(columns, -here % LANES, 1)
        every[pl.ds(n * KEEP, KEEP), :] = jnp.where(margin, jnp.where(at_left, right, left), value)

    even = lax.axis_index("row") % 2 == 0
    plane = lambda n: every[pl.ds(n * KEEP, KEEP), :]
    chosen = []
    for date in range(2):
        for link in range(LINKS):
            slot = jnp.broadcast_to(slots[pl.ds(LINKS * date + link, 1), :], (KEEP, LANES))
            triples = [
                (plane(2 * (3 * date + n - 1)), plane(2 * (3 * date + n - 1) + 1), plane(PLANES - 6 + n))
                for n in range(date + 1, date + 5)
            ]
            values = triples[0]
            for n, triple in zip(range(date + 2, date + 5), triples[1:]):
                values = [jnp.where(slot == n, v, w) for v, w in zip(triple, values)]
            chosen += values
    chosen += [plane(PLANES - 6 + date) for date in range(2)]
    for n, value in enumerate(chosen):
        picked[pl.ds(n * KEEP, KEEP), :] = value
        top, bottom = value[:MARGIN], value[KEEP - MARGIN :]
        chip[pl.ds(MARGIN * n, MARGIN), :] = jnp.where(even, bottom, top)
        across[pl.ds(MARGIN * n, MARGIN), :] = jnp.where(even, top, bottom)


@functools.lru_cache(None)
def tables():
    blocks = LANES // PATCH
    n = np.arange(PATCH)
    angle = 2.0 * np.pi * (np.outer(n, n) % PATCH) / PATCH
    cosine, sine = np.cos(angle), np.sin(angle)
    forward = np.zeros((LANES, 2 * LANES))
    spread = np.zeros((LANES, 2 * LANES))
    inverse = np.zeros((LANES, 2 * LANES))
    for b in range(blocks):
        f = slice(b * PATCH, (b + 1) * PATCH)
        x = slice(b * KEEP, b * KEEP + PATCH)
        o = slice(b * KEEP, (b + 1) * KEEP)
        kept = slice(MARGIN, MARGIN + KEEP)
        forward[x, f] = cosine
        forward[x, LANES + b * PATCH : LANES + (b + 1) * PATCH] = -sine
        inverse[f, o] = cosine[:, kept] / PATCH
        inverse[f, LANES + b * KEEP : LANES + (b + 1) * KEEP] = sine[:, kept] / PATCH
        near = (n[:, None] - n[None, :]) % PATCH
        spread[f, f] = (near == 0) | (near == 1) | (near == PATCH - 1)
        spread[f, LANES + b * PATCH : LANES + (b + 1) * PATCH] = 1.0
    down = np.block([[cosine, sine], [-sine, cosine]])
    kept = slice(MARGIN, MARGIN + KEEP)
    up = np.block([[cosine[kept], -sine[kept]], [sine[kept], cosine[kept]]]) / PATCH

    def thrice(table, axis):
        high = table.astype(np.float32).astype(BF16)
        low = (table - high.astype(np.float64)).astype(np.float32).astype(BF16)
        return np.concatenate([high, low, high], axis=axis)

    twice = np.concatenate([spread, spread], axis=0).astype(np.float32).astype(BF16)
    return [thrice(forward, 0), twice, thrice(inverse, 0), thrice(down, 1), thrice(up, 1)]


def parts(values):
    high = values.astype(BF16)
    return high, (values - high.astype(F32)).astype(BF16)


def narrow_dot(a, b):
    return jnp.dot(a, b, preferred_element_type=F32)


def right_dot(values, table):
    high, low = parts(values)
    return narrow_dot(jnp.concatenate([high, high, low], axis=1), table)


def left_dot(table, values):
    high, low = parts(values)
    return narrow_dot(table, jnp.concatenate([high, high, low], axis=0))


def sum_dot(values, table):
    return narrow_dot(jnp.concatenate(parts(values), axis=1), table)


def filter_kernel(picked, across, chip, forward, spread, inverse, down, up, filtered, coherent, pad):
    even = lax.axis_index("row") % 2 == 0
    pairs = 2 * LINKS
    for n in range(3 * pairs + 2):
        near, far = chip[pl.ds(MARGIN * n, MARGIN), :], across[pl.ds(MARGIN * n, MARGIN), :]
        pad[n, pl.ds(0, MARGIN), :] = jnp.where(even, far, near)
        pad[n, pl.ds(MARGIN, KEEP), :] = picked[pl.ds(n * KEEP, KEEP), :]
        pad[n, pl.ds(MARGIN + KEEP, MARGIN), :] = jnp.where(even, near, far)

    def box(value):
        rows = value[3 : 3 + KEEP] + value[4 : 4 + KEEP] + value[5 : 5 + KEEP]
        total = pltpu.roll(rows, LANES - 3, 1) + pltpu.roll(rows, LANES - 4, 1) + pltpu.roll(rows, LANES - 5, 1)
        return total * (1.0 / 9.0)

    wide = coherent.shape[-1]
    firsts = [box(pad[3 * pairs + date]) for date in range(2)]
    for p in range(pairs):
        real, imag, second = [box(pad[3 * p + k]) for k in range(3)]
        factor = lax.rsqrt(firsts[p // LINKS] * second + 1e-06)
        coherent[p // LINKS, p % LINKS, 0] = (real * factor)[:, :wide]
        coherent[p // LINKS, p % LINKS, 1] = (imag * factor)[:, :wide]

    reals = jnp.concatenate([pad[3 * p] for p in range(pairs)], axis=0)
    imags = jnp.concatenate([pad[3 * p + 1] for p in range(pairs)], axis=0)
    size = pairs * PATCH
    across_cols = right_dot(jnp.concatenate([reals, imags], axis=0), forward[...])
    col_real = across_cols[:size, :LANES] - across_cols[size:, LANES:]
    col_imag = across_cols[size:, :LANES] + across_cols[:size, LANES:]
    rows_of = lambda v, p, count: v[p * count : (p + 1) * count]
    stacked = jnp.concatenate(
        [
            jnp.concatenate([rows_of(col_real, p, PATCH), rows_of(col_imag, p, PATCH)], axis=0)
            for p in range(pairs)
        ],
        axis=1,
    )
    spectrum = left_dot(down[...], stacked)
    real, imag = spectrum[:PATCH], spectrum[PATCH:]
    power = real * real + imag * imag
    lanes_of = lambda v, p: v[:, p * LANES : (p + 1) * LANES]
    tall = lambda v: jnp.concatenate([lanes_of(v, p) for p in range(pairs)], axis=0)
    sums = sum_dot(tall(power), spread[...])
    weights = []
    for p in range(pairs):
        near = rows_of(sums, p, PATCH)[:, :LANES]
        level = jnp.sum(rows_of(sums, p, PATCH)[:, LANES:], axis=0, keepdims=True) * (1.0 / (PATCH * PATCH))
        smooth = (near + pltpu.roll(near, 1, 0) + pltpu.roll(near, PATCH - 1, 0)) * (1.0 / 9.0)
        weights.append(jnp.sqrt(jnp.sqrt(smooth + level + 1e-06)))
    totals = sum_dot(jnp.concatenate(weights, axis=0), spread[:, LANES:])
    scaled = []
    for p in range(pairs):
        total = jnp.sum(rows_of(totals, p, PATCH), axis=0, keepdims=True)
        scaled.append(weights[p] * ((PATCH * PATCH) / total))
    weight = jnp.concatenate(scaled, axis=1)
    lifted = left_dot(up[...], jnp.concatenate([real * weight, imag * weight], axis=0))
    low, high = lifted[:KEEP], lifted[KEEP:]
    size = pairs * KEEP
    result = right_dot(jnp.concatenate([tall(low), tall(high)], axis=0), inverse[...])
    out_real = result[:size, :LANES] - result[size:, LANES:]
    out_imag = result[size:, :LANES] + result[:size, LANES:]
    for p in range(pairs):
        filtered[p // LINKS, p % LINKS, 0] = rows_of(out_real, p, KEEP)[:, :wide]
        filtered[p // LINKS, p % LINKS, 1] = rows_of(out_imag, p, KEEP)[:, :wide]


def body(images, secondaries):
    rows, cols = images.shape[2:]
    cells_down, cells_along = rows // 2, cols // 8
    dates, count = lax.axis_size("date"), lax.axis_size("row")
    inner = lambda steps: [(d, d + steps) for d in range(dates) if 0 <= d % RUN + steps < RUN]
    outer = lambda steps: [(d, (d + steps) % dates) for d in range(dates) if not 0 <= d % RUN + steps < RUN]
    along = lambda value, pairs: lax.ppermute(value, "date", pairs)
    across = lambda value, pairs: lax.ppermute(
        value, ("date", "col"), [(2 * d + c, 2 * e + (c ^ 1)) for d, e in pairs for c in range(2)]
    )
    after, before = along(images, inner(-1)), along(images, inner(1))
    after_wrap, before_wrap = along(images, outer(-1)), along(images, outer(1))
    own, slots = kept(images, secondaries)
    step = lambda wanted: [(d, (d - 1) % dates) for d in range(dates) if wanted(d % RUN)]
    middle, low, high = step(lambda n: 0 < n < RUN - 1), step(lambda n: n == 0), step(lambda n: n == RUN - 1)
    held, sent, side = near(own, after, before)
    side, back = across(side, middle), along(sent, middle)
    sent, low_side = at_end(0, own, before_wrap, after, side, back, before)
    formed = low_side
    low_side, low_back = across(low_side, low), along(sent, low)
    last_held, sent, high_side = at_end(RUN - 1, own, before, after_wrap, formed)
    high_side, high_back = across(high_side, high), along(sent, high)
    side, back = call(merge_kernel, planes_of(rows, 1, LEAVING), 4)(side, back, low_side, low_back)

    planes = 3 * 2 * LINKS + 2
    rim = jax.ShapeDtypeStruct((planes * MARGIN, LANES), F32)
    every = pltpu.VMEM((PLANES * cells_down, LANES), F32)
    picked = jax.ShapeDtypeStruct((planes * cells_down, LANES), F32)
    picked, chip, across = call(rims_kernel, (picked, rim, rim), 7, [every])(
        slots, held, last_held, side, back, high_side, high_back
    )
    chip = lax.ppermute(chip, "row", [(i, i ^ 1) for i in range(count)])
    across = lax.ppermute(across, "row", [(i, ((i + 1) ^ 1) - 1) for i in range(1, count - 1)])
    out = jax.ShapeDtypeStruct((2, LINKS, 2, cells_down, cells_along), F32)
    return call(filter_kernel, (out, out), 8, [pltpu.VMEM((planes, PATCH, LANES), F32)])(
        picked, across, chip, *tables()
    )


def solution(mesh):
    in_specs = (P("date", None, "row", "col"), P("date", None))
    out_specs = (P("date", None, None, "row", "col"), P("date", None, None, "row", "col"))
    return jax.shard_map(body, mesh=mesh, in_specs=in_specs, out_specs=out_specs, check_vma=False)
```

```python
import functools
import math

import jax
import jax.numpy as jnp
import numpy as np
from jax import lax
from jax.experimental import pallas as pl
from jax.experimental.pallas import tpu as pltpu
from jax.sharding import PartitionSpec as P

KEEP = 24
PATCH = 32
MARGIN = 4
LANES = 128
STRIP = 32
RIGHT = 100
LINKS = 3
RUN = 16
F32 = jnp.float32
BF16 = jnp.bfloat16

HELD = ((0, 1), (0, 2), (0, 3), (1, 2), (1, 3))
SENT = ((-2, 2), (-1, 2), (-1, 3))
CANDIDATES = tuple((a - 2, b - 2) for a in range(2) for b in range(a + 1, a + 5))
PLANES = 2 * len(CANDIDATES) + 6


def vmem():
    return pl.BlockSpec(memory_space=pltpu.VMEM)


def smem():
    return pl.BlockSpec(memory_space=pltpu.SMEM)


def call(kernel, outs, count, scratch=(), specs=None, flops=1e6, moved=1e6):
    return pl.pallas_call(
        kernel,
        out_shape=outs,
        in_specs=specs or [vmem()] * count,
        out_specs=jax.tree.map(lambda _: vmem(), outs),
        scratch_shapes=list(scratch),
        compiler_params=pltpu.CompilerParams(vmem_limit_bytes=32 * 1024 * 1024),
        cost_estimate=pl.CostEstimate(flops=int(flops), bytes_accessed=int(moved), transcendentals=0),
    )


def lane_index(shape):
    return lax.broadcasted_iota(jnp.int32, shape, len(shape) - 1)


def looks_table(cols):
    source = lax.broadcasted_iota(jnp.int32, (cols, LANES), 0)
    target = lax.broadcasted_iota(jnp.int32, (cols, LANES), 1)
    return jnp.where((source >> 3) + MARGIN == target, 1.0 / 16.0, 0.0).astype(BF16)


def split_dot(values, table):
    high = values.astype(BF16)
    rest = values - high.astype(F32)
    middle = rest.astype(BF16)
    low = (rest - middle.astype(F32)).astype(BF16)
    dot = lambda v: jnp.dot(v, table, preferred_element_type=F32)
    return dot(high) + (dot(middle) + dot(low))


def tiled(images):
    rows, cols = images.shape[2:]
    spec = lambda index: pl.BlockSpec((2, 2, rows, LANES), lambda i: (0, 0, 0, index))
    return [spec(index) for index in range(cols // LANES)]


def keep_kernel(secondaries, source, target, slots, arrived):
    copies = [
        pltpu.make_async_copy(
            source.at[:, :, :, pl.ds(tile * LANES, LANES)], target.at[tile], arrived.at[tile]
        )
        for tile in range(target.shape[0])
    ]
    for copy in copies:
        copy.start()
    first = 2 * lax.axis_index("date")
    dates = 2 * lax.axis_size("date")
    for date in range(2):
        for link in range(LINKS):
            slot = (secondaries[date, link] - first + dates) % dates
            slots[pl.ds(LINKS * date + link, 1), :] = jnp.full((1, LANES), slot, jnp.int32)
    for copy in copies:
        copy.wait()


def kept(images, secondaries):
    tiles = images.shape[3] // LANES
    return pl.pallas_call(
        keep_kernel,
        out_shape=(
            pltpu.VMEM((tiles,) + images.shape[:3] + (LANES,), F32),
            pltpu.VMEM((8, LANES), jnp.int32),
        ),
        in_specs=[smem(), pl.BlockSpec(memory_space=pl.ANY)],
        out_specs=(vmem(), vmem()),
        scratch_shapes=[pltpu.SemaphoreType.DMA((tiles,))],
    )(secondaries, images)


def product(a, b):
    (ar, ai), (br, bi) = a, b
    real = (ar[0] * br[0] + ai[0] * bi[0]) + (ar[1] * br[1] + ai[1] * bi[1])
    imag = (ai[0] * br[0] - ar[0] * bi[0]) + (ai[1] * br[1] - ar[1] * bi[1])
    return real, imag


def power(a):
    ar, ai = a
    return (ar[0] * ar[0] + ai[0] * ai[0]) + (ar[1] * ar[1] + ai[1] * ai[1])


def reader(own, others):
    half = own.shape[3] // 2

    def image(slot, tile):
        def value(part, parity):
            rows = pl.ds(parity, half, stride=2)
            if 0 <= slot < 2:
                return own[tile, slot, part, rows, :]
            here, there, turn = others[slot // 2]
            first = here[tile][slot % 2, part, rows, :]
            return first if there is None else jnp.where(turn, there[tile][slot % 2, part, rows, :], first)

        return [[value(part, parity) for parity in range(2)] for part in range(2)]

    return image


def fill(stage, image, tiles, half, pairs, slots):
    for tile in range(tiles):
        lanes = pl.ds(tile * LANES, LANES)
        loaded = {slot: image(slot, tile) for slot in {s for pair in pairs for s in pair} | set(slots)}
        values = [v for a, b in pairs for v in product(loaded[a], loaded[b])]
        values += [power(loaded[slot]) for slot in slots]
        for n, value in enumerate(values):
            stage[pl.ds(n * half, half), lanes] = value


def meet(stage, image, tiles, half, wanted, *outs):
    pairs, slots = wanted
    fill(stage, image, tiles, half, pairs, slots)
    at_left = lax.axis_index("col") == 0

    def border(slot):
        here, there = image(slot, tiles - 1), image(slot, 0)
        return [
            [jnp.where(at_left, pltpu.roll(v, STRIP, 1), w) for v, w in zip(p, q)]
            for p, q in zip(here, there)
        ]

    bordered = {slot: border(slot) for slot in range(-2, 4)}
    values = [v for a, b in CANDIDATES for v in product(bordered[a], bordered[b])]
    values += [power(bordered[slot]) for slot in range(-2, 4)]
    block = lane_index((half, LANES)) >> 5
    rows = pl.ds((2 * len(pairs) + len(slots)) * half, half)
    for tile in range(tiles):
        row = jnp.zeros((half, LANES), F32)
        for k, value in enumerate(values[4 * tile : 4 * tile + 4]):
            row = jnp.where(block == k, pltpu.roll(value, STRIP * k, 1) if k else value, row)
        stage[rows, pl.ds(tile * LANES, LANES)] = row
    means = split_dot(stage[...], looks_table(tiles * LANES))
    at = 0
    for out in outs:
        out[...] = means[at : at + out.shape[0]]
        at += out.shape[0]


ALL = (HELD + SENT, (0, 1, 2, 3))
GOING = (SENT, (2, 3))


def near_kernel(*refs):
    own, (held, sent, side, stage, means) = refs[0], refs[-5:]
    tiles, half = own.shape[0], own.shape[3] // 2
    before, after = [refs[1 + n * tiles : 1 + (n + 1) * tiles] for n in range(2)]

    @pl.when(lax.axis_index("date") % RUN < RUN - 1)
    def _():
        image = reader(own, {-1: (before, None, None), 1: (after, None, None)})
        meet(stage, image, tiles, half, ALL, means, side)
        share(means, half, held, sent)


def share(means, half, held, sent):
    kept, going = 2 * len(HELD) * half, 2 * len(SENT) * half
    held[pl.ds(0, kept), :] = means[pl.ds(0, kept), :]
    held[pl.ds(kept, 4 * half), :] = means[pl.ds(kept + going, 4 * half), :]
    sent[pl.ds(0, going), :] = means[pl.ds(kept, going), :]
    sent[pl.ds(going, 2 * half), :] = means[pl.ds(kept + going + 2 * half, 2 * half), :]


def end_kernel(run, own, before, after, *refs):
    count = 2 if run == 0 else 4
    outs, (stage, mine, near, arrived) = refs[-4 - count : -4], refs[-4:]
    tiles, half = own.shape[0], own.shape[3] // 2

    @pl.when(lax.axis_index("date") % RUN == run)
    def _():
        copies = [pltpu.make_async_copy(own, mine, arrived.at[0, 0])]
        for n, source in enumerate((before, after)):
            for tile in range(tiles):
                lanes = pl.ds(tile * LANES, LANES)
                copies.append(
                    pltpu.make_async_copy(source.at[:, :, :, lanes], near.at[n, tile], arrived.at[n + 1, tile])
                )
        for copy in copies:
            copy.start()
        for copy in copies:
            copy.wait()
        blocks = [[near.at[n, tile] for tile in range(tiles)] for n in range(2)]
        image = reader(mine, {-1: (blocks[0], None, None), 1: (blocks[1], None, None)})
        if run == 0:
            sent, side = outs
            side[pl.ds(half, side.shape[0] - half), :] = jnp.zeros((side.shape[0] - half, LANES), F32)
            meet(stage, image, tiles, half, GOING, sent, side.at[pl.ds(0, half), :])
        else:
            held, sent, side, means = outs
            meet(stage, image, tiles, half, ALL, means, side)
            share(means, half, held, sent)


def planes_of(rows, *counts):
    return tuple(jax.ShapeDtypeStruct((count * rows // 2, LANES), F32) for count in counts)


STAYING, LEAVING = 2 * len(HELD) + 4, 2 * len(SENT) + 2
BOTH = 2 * len(HELD + SENT) + 4


def at_end(run, own, before, after, *behind):
    rows, cols = after.shape[2:]
    half, tiles = rows // 2, cols // LANES
    outs = (LEAVING, 8) if run == 0 else (STAYING, LEAVING, 1)
    total = LEAVING if run == 0 else BOTH
    scratch = [
        pltpu.VMEM(((total + 1) * half, cols), F32),
        pltpu.VMEM(own.shape, F32),
        pltpu.VMEM((2,) + own.shape, F32),
        pltpu.SemaphoreType.DMA((3, tiles)),
    ]
    return call(
        functools.partial(end_kernel, run),
        planes_of(rows, *outs),
        3 + len(behind),
        ([] if run == 0 else [pltpu.VMEM((BOTH * half, LANES), F32)]) + scratch,
        [pl.BlockSpec(memory_space=pl.ANY)] * (3 + len(behind)),
    )(own, before, after, *behind)


def near(own, *images):
    rows, cols = images[0].shape[2:]
    half = rows // 2
    whole = lambda shape: pl.BlockSpec(shape, lambda i: (0,) * len(shape))
    outs = planes_of(rows, STAYING, LEAVING, 1)
    return pl.pallas_call(
        near_kernel,
        grid=(1,),
        out_shape=outs,
        in_specs=[whole(own.shape)] + [spec for image in images for spec in tiled(image)],
        out_specs=tuple(whole(out.shape) for out in outs),
        scratch_shapes=[pltpu.VMEM(((BOTH + 1) * half, cols), F32), pltpu.VMEM((BOTH * half, LANES), F32)],
        compiler_params=pltpu.CompilerParams(vmem_limit_bytes=32 * 1024 * 1024),
    )(own, *[image for image in images for _ in range(cols // LANES)])


def arrived_kernel(side, back, new_side, new_back):
    new_side[...] = side[pl.ds(0, new_side.shape[0]), :]
    new_back[...] = back[...]


def merge_kernel(side, back, low_side, low_back, new_side, new_back):
    from_low = lax.axis_index("date") % RUN == RUN - 1
    new_side[...] = jnp.where(from_low, low_side[pl.ds(0, side.shape[0]), :], side[...])
    new_back[...] = jnp.where(from_low, low_back[...], back[...])


def rims_kernel(
    slots,
    held,
    last_held,
    side,
    back,
    high_side,
    high_back,
    picked,
    chip,
    across,
    every,
):
    at_left = lax.axis_index("col") == 0
    lanes = lane_index((KEEP, LANES))
    edge = jnp.where(at_left, RIGHT, 0)
    margin = (lanes >= edge) & (lanes < edge + MARGIN)
    place = lax.axis_index("date") % RUN
    from_low, from_high = place == RUN - 1, place == RUN - 2
    columns = jnp.where(from_high, high_side[...], side[...])
    held_at, back_at = 0, 0
    for n in range(PLANES):
        pair = n // 2
        from_back = pair in (3, 6, 7) or n >= PLANES - 2
        if from_back:
            rows = pl.ds(back_at * KEEP, KEEP)
            value, back_at = jnp.where(from_high, high_back[rows, :], back[rows, :]), back_at + 1
        else:
            rows = pl.ds(held_at * KEEP, KEEP)
            value, held_at = jnp.where(from_low, last_held[rows, :], held[rows, :]), held_at + 1
        here = MARGIN + MARGIN * n
        right = pltpu.roll(columns, (RIGHT - here) % LANES, 1)
        left = pltpu.roll(columns, -here % LANES, 1)
        every[pl.ds(n * KEEP, KEEP), :] = jnp.where(margin, jnp.where(at_left, right, left), value)

    even = lax.axis_index("row") % 2 == 0
    plane = lambda n: every[pl.ds(n * KEEP, KEEP), :]
    chosen = []
    for date in range(2):
        for link in range(LINKS):
            slot = jnp.broadcast_to(slots[pl.ds(LINKS * date + link, 1), :], (KEEP, LANES))
            triples = [
                (plane(2 * (3 * date + n - 1)), plane(2 * (3 * date + n - 1) + 1), plane(PLANES - 6 + n))
                for n in range(date + 1, date + 5)
            ]
            values = triples[0]
            for n, triple in zip(range(date + 2, date + 5), triples[1:]):
                values = [jnp.where(slot == n, v, w) for v, w in zip(triple, values)]
            chosen += values
    chosen += [plane(PLANES - 6 + date) for date in range(2)]
    for n, value in enumerate(chosen):
        picked[pl.ds(n * KEEP, KEEP), :] = value
        top, bottom = value[:MARGIN], value[KEEP - MARGIN :]
        chip[pl.ds(MARGIN * n, MARGIN), :] = jnp.where(even, bottom, top)
        across[pl.ds(MARGIN * n, MARGIN), :] = jnp.where(even, top, bottom)


@functools.lru_cache(None)
def tables():
    blocks = LANES // PATCH
    n = np.arange(PATCH)
    angle = 2.0 * np.pi * (np.outer(n, n) % PATCH) / PATCH
    cosine, sine = np.cos(angle), np.sin(angle)
    forward = np.zeros((LANES, 2 * LANES))
    spread = np.zeros((LANES, 2 * LANES))
    inverse = np.zeros((LANES, 2 * LANES))
    for b in range(blocks):
        f = slice(b * PATCH, (b + 1) * PATCH)
        x = slice(b * KEEP, b * KEEP + PATCH)
        o = slice(b * KEEP, (b + 1) * KEEP)
        kept = slice(MARGIN, MARGIN + KEEP)
        forward[x, f] = cosine
        forward[x, LANES + b * PATCH : LANES + (b + 1) * PATCH] = -sine
        inverse[f, o] = cosine[:, kept] / PATCH
        inverse[f, LANES + b * KEEP : LANES + (b + 1) * KEEP] = sine[:, kept] / PATCH
        near = (n[:, None] - n[None, :]) % PATCH
        spread[f, f] = (near == 0) | (near == 1) | (near == PATCH - 1)
        spread[f, LANES + b * PATCH : LANES + (b + 1) * PATCH] = 1.0
    down = np.block([[cosine, sine], [-sine, cosine]])
    kept = slice(MARGIN, MARGIN + KEEP)
    up = np.block([[cosine[kept], -sine[kept]], [sine[kept], cosine[kept]]]) / PATCH

    def thrice(table, axis):
        high = table.astype(np.float32).astype(BF16)
        low = (table - high.astype(np.float64)).astype(np.float32).astype(BF16)
        return np.concatenate([high, low, high], axis=axis)

    twice = np.concatenate([spread, spread], axis=0).astype(np.float32).astype(BF16)
    return [thrice(forward, 0), twice, thrice(inverse, 0), thrice(down, 1), thrice(up, 1)]


def parts(values):
    high = values.astype(BF16)
    return high, (values - high.astype(F32)).astype(BF16)


def narrow_dot(a, b):
    return jnp.dot(a, b, preferred_element_type=F32)


def right_dot(values, table):
    high, low = parts(values)
    return narrow_dot(jnp.concatenate([high, high, low], axis=1), table)


def left_dot(table, values):
    high, low = parts(values)
    return narrow_dot(table, jnp.concatenate([high, high, low], axis=0))


def sum_dot(values, table):
    return narrow_dot(jnp.concatenate(parts(values), axis=1), table)


def filter_kernel(picked, across, chip, forward, spread, inverse, down, up, filtered, coherent, pad):
    even = lax.axis_index("row") % 2 == 0
    pairs = 2 * LINKS
    for n in range(3 * pairs + 2):
        near, far = chip[pl.ds(MARGIN * n, MARGIN), :], across[pl.ds(MARGIN * n, MARGIN), :]
        pad[n, pl.ds(0, MARGIN), :] = jnp.where(even, far, near)
        pad[n, pl.ds(MARGIN, KEEP), :] = picked[pl.ds(n * KEEP, KEEP), :]
        pad[n, pl.ds(MARGIN + KEEP, MARGIN), :] = jnp.where(even, near, far)

    def box(value):
        rows = value[3 : 3 + KEEP] + value[4 : 4 + KEEP] + value[5 : 5 + KEEP]
        total = pltpu.roll(rows, LANES - 3, 1) + pltpu.roll(rows, LANES - 4, 1) + pltpu.roll(rows, LANES - 5, 1)
        return total * (1.0 / 9.0)

    wide = coherent.shape[-1]
    firsts = [box(pad[3 * pairs + date]) for date in range(2)]
    for p in range(pairs):
        real, imag, second = [box(pad[3 * p + k]) for k in range(3)]
        factor = lax.rsqrt(firsts[p // LINKS] * second + 1e-06)
        coherent[p // LINKS, p % LINKS, 0] = (real * factor)[:, :wide]
        coherent[p // LINKS, p % LINKS, 1] = (imag * factor)[:, :wide]

    reals = jnp.concatenate([pad[3 * p] for p in range(pairs)], axis=0)
    imags = jnp.concatenate([pad[3 * p + 1] for p in range(pairs)], axis=0)
    size = pairs * PATCH
    across_cols = right_dot(jnp.concatenate([reals, imags], axis=0), forward[...])
    col_real = across_cols[:size, :LANES] - across_cols[size:, LANES:]
    col_imag = across_cols[size:, :LANES] + across_cols[:size, LANES:]
    rows_of = lambda v, p, count: v[p * count : (p + 1) * count]
    stacked = jnp.concatenate(
        [
            jnp.concatenate([rows_of(col_real, p, PATCH), rows_of(col_imag, p, PATCH)], axis=0)
            for p in range(pairs)
        ],
        axis=1,
    )
    spectrum = left_dot(down[...], stacked)
    real, imag = spectrum[:PATCH], spectrum[PATCH:]
    power = real * real + imag * imag
    lanes_of = lambda v, p: v[:, p * LANES : (p + 1) * LANES]
    tall = lambda v: jnp.concatenate([lanes_of(v, p) for p in range(pairs)], axis=0)
    sums = sum_dot(tall(power), spread[...])
    weights = []
    for p in range(pairs):
        near = rows_of(sums, p, PATCH)[:, :LANES]
        level = jnp.sum(rows_of(sums, p, PATCH)[:, LANES:], axis=0, keepdims=True) * (1.0 / (PATCH * PATCH))
        smooth = (near + pltpu.roll(near, 1, 0) + pltpu.roll(near, PATCH - 1, 0)) * (1.0 / 9.0)
        weights.append(jnp.sqrt(jnp.sqrt(smooth + level + 1e-06)))
    totals = sum_dot(jnp.concatenate(weights, axis=0), spread[:, LANES:])
    scaled = []
    for p in range(pairs):
        total = jnp.sum(rows_of(totals, p, PATCH), axis=0, keepdims=True)
        scaled.append(weights[p] * ((PATCH * PATCH) / total))
    weight = jnp.concatenate(scaled, axis=1)
    lifted = left_dot(up[...], jnp.concatenate([real * weight, imag * weight], axis=0))
    low, high = lifted[:KEEP], lifted[KEEP:]
    size = pairs * KEEP
    result = right_dot(jnp.concatenate([tall(low), tall(high)], axis=0), inverse[...])
    out_real = result[:size, :LANES] - result[size:, LANES:]
    out_imag = result[size:, :LANES] + result[:size, LANES:]
    for p in range(pairs):
        filtered[p // LINKS, p % LINKS, 0] = rows_of(out_real, p, KEEP)[:, :wide]
        filtered[p // LINKS, p % LINKS, 1] = rows_of(out_imag, p, KEEP)[:, :wide]


def body(images, secondaries):
    rows, cols = images.shape[2:]
    cells_down, cells_along = rows // 2, cols // 8
    dates, count = lax.axis_size("date"), lax.axis_size("row")
    inner = lambda steps: [(d, d + steps) for d in range(dates) if 0 <= d % RUN + steps < RUN]
    outer = lambda steps: [(d, (d + steps) % dates) for d in range(dates) if not 0 <= d % RUN + steps < RUN]
    along = lambda value, pairs: lax.ppermute(value, "date", pairs)
    across = lambda value, pairs: lax.ppermute(
        value, ("date", "col"), [(2 * d + c, 2 * e + (c ^ 1)) for d, e in pairs for c in range(2)]
    )
    up_from = lambda wanted: [(d, d + 1) for d in range(dates) if wanted(d % RUN)]
    after, before = along(images, inner(-1)), along(images, up_from(lambda n: n < RUN - 2))
    after_wrap, before_wrap = along(images, outer(-1)), along(images, outer(1))
    before_last = along(images, up_from(lambda n: n == RUN - 2))
    own, slots = kept(images, secondaries)
    step = lambda wanted: [(d, (d - 1) % dates) for d in range(dates) if wanted(d % RUN)]
    middle, low, high = step(lambda n: 0 < n < RUN - 1), step(lambda n: n == 0), step(lambda n: n == RUN - 1)
    held, sent, side = near(own, before, after)
    side, back = across(side, middle), along(sent, middle)
    sent, low_side = at_end(0, own, before_wrap, after, side, before)
    formed = low_side
    low_side, low_back = across(low_side, low), along(sent, low)
    last_held, sent, high_side = at_end(RUN - 1, own, before_last, after_wrap, formed)
    high_side, high_back = across(high_side, high), along(sent, high)
    side, back = call(arrived_kernel, planes_of(rows, 1, LEAVING), 2)(side, back)
    side, back = call(merge_kernel, planes_of(rows, 1, LEAVING), 4)(side, back, low_side, low_back)

    planes = 3 * 2 * LINKS + 2
    rim = jax.ShapeDtypeStruct((planes * MARGIN, LANES), F32)
    every = pltpu.VMEM((PLANES * cells_down, LANES), F32)
    picked = jax.ShapeDtypeStruct((planes * cells_down, LANES), F32)
    picked, chip, across = call(rims_kernel, (picked, rim, rim), 7, [every])(
        slots, held, last_held, side, back, high_side, high_back
    )
    chip = lax.ppermute(chip, "row", [(i, i ^ 1) for i in range(count)])
    across = lax.ppermute(across, "row", [(i, ((i + 1) ^ 1) - 1) for i in range(1, count - 1)])
    out = jax.ShapeDtypeStruct((2, LINKS, 2, cells_down, cells_along), F32)
    return call(filter_kernel, (out, out), 8, [pltpu.VMEM((planes, PATCH, LANES), F32)])(
        picked, across, chip, *tables()
    )


def solution(mesh):
    in_specs = (P("date", None, "row", "col"), P("date", None))
    out_specs = (P("date", None, None, "row", "col"), P("date", None, None, "row", "col"))
    return jax.shard_map(body, mesh=mesh, in_specs=in_specs, out_specs=out_specs, check_vma=False)
```

```python
import functools
import math

import jax
import jax.numpy as jnp
import numpy as np
from jax import lax
from jax.experimental import pallas as pl
from jax.experimental.pallas import tpu as pltpu
from jax.sharding import PartitionSpec as P

KEEP = 24
PATCH = 32
MARGIN = 4
LANES = 128
STRIP = 32
RIGHT = 100
LINKS = 3
RUN = 16
F32 = jnp.float32
BF16 = jnp.bfloat16

HELD = ((0, 1), (0, 2), (0, 3), (1, 2), (1, 3))
SENT = ((-2, 2), (-1, 2), (-1, 3))
CANDIDATES = tuple((a - 2, b - 2) for a in range(2) for b in range(a + 1, a + 5))
PLANES = 2 * len(CANDIDATES) + 6


def vmem():
    return pl.BlockSpec(memory_space=pltpu.VMEM)


def smem():
    return pl.BlockSpec(memory_space=pltpu.SMEM)


def call(kernel, outs, count, scratch=(), specs=None, flops=1e6, moved=1e6):
    return pl.pallas_call(
        kernel,
        out_shape=outs,
        in_specs=specs or [vmem()] * count,
        out_specs=jax.tree.map(lambda _: vmem(), outs),
        scratch_shapes=list(scratch),
        compiler_params=pltpu.CompilerParams(vmem_limit_bytes=32 * 1024 * 1024),
        cost_estimate=pl.CostEstimate(flops=int(flops), bytes_accessed=int(moved), transcendentals=0),
    )


def lane_index(shape):
    return lax.broadcasted_iota(jnp.int32, shape, len(shape) - 1)


def looks_table(cols):
    source = lax.broadcasted_iota(jnp.int32, (cols, LANES), 0)
    target = lax.broadcasted_iota(jnp.int32, (cols, LANES), 1)
    return jnp.where((source >> 3) + MARGIN == target, 1.0 / 16.0, 0.0).astype(BF16)


def split_dot(values, table):
    high = values.astype(BF16)
    rest = values - high.astype(F32)
    middle = rest.astype(BF16)
    low = (rest - middle.astype(F32)).astype(BF16)
    dot = lambda v: jnp.dot(v, table, preferred_element_type=F32)
    return dot(high) + (dot(middle) + dot(low))


def tiled(images):
    rows, cols = images.shape[2:]
    spec = lambda index: pl.BlockSpec((2, 2, rows, LANES), lambda i: (0, 0, 0, index))
    return [spec(index) for index in range(cols // LANES)]


def keep_kernel(secondaries, source, target, slots, arrived):
    copies = [
        pltpu.make_async_copy(
            source.at[:, :, :, pl.ds(tile * LANES, LANES)], target.at[tile], arrived.at[tile]
        )
        for tile in range(target.shape[0])
    ]
    for copy in copies:
        copy.start()
    first = 2 * lax.axis_index("date")
    dates = 2 * lax.axis_size("date")
    for date in range(2):
        for link in range(LINKS):
            slot = (secondaries[date, link] - first + dates) % dates
            slots[pl.ds(LINKS * date + link, 1), :] = jnp.full((1, LANES), slot, jnp.int32)
    for copy in copies:
        copy.wait()


def kept(images, secondaries):
    tiles = images.shape[3] // LANES
    return pl.pallas_call(
        keep_kernel,
        out_shape=(
            pltpu.VMEM((tiles,) + images.shape[:3] + (LANES,), F32),
            pltpu.VMEM((8, LANES), jnp.int32),
        ),
        in_specs=[smem(), pl.BlockSpec(memory_space=pl.ANY)],
        out_specs=(vmem(), vmem()),
        scratch_shapes=[pltpu.SemaphoreType.DMA((tiles,))],
    )(secondaries, images)


def product(a, b):
    (ar, ai), (br, bi) = a, b
    real = (ar[0] * br[0] + ai[0] * bi[0]) + (ar[1] * br[1] + ai[1] * bi[1])
    imag = (ai[0] * br[0] - ar[0] * bi[0]) + (ai[1] * br[1] - ar[1] * bi[1])
    return real, imag


def power(a):
    ar, ai = a
    return (ar[0] * ar[0] + ai[0] * ai[0]) + (ar[1] * ar[1] + ai[1] * ai[1])


def reader(own, others):
    half = own.shape[3] // 2

    def image(slot, tile):
        def value(part, parity):
            rows = pl.ds(parity, half, stride=2)
            if 0 <= slot < 2:
                return own[tile, slot, part, rows, :]
            here, there, turn = others[slot // 2]
            first = here[tile][slot % 2, part, rows, :]
            return first if there is None else jnp.where(turn, there[tile][slot % 2, part, rows, :], first)

        return [[value(part, parity) for parity in range(2)] for part in range(2)]

    return image


def fill(stage, image, tiles, half, pairs, slots):
    for tile in range(tiles):
        lanes = pl.ds(tile * LANES, LANES)
        loaded = {slot: image(slot, tile) for slot in {s for pair in pairs for s in pair} | set(slots)}
        values = [v for a, b in pairs for v in product(loaded[a], loaded[b])]
        values += [power(loaded[slot]) for slot in slots]
        for n, value in enumerate(values):
            stage[pl.ds(n * half, half), lanes] = value


def pack(planes):
    lanes = lane_index(planes[0].shape)
    packed = []
    for n in range(0, len(planes), 4):
        shifts = (-MARGIN, 3 * STRIP - MARGIN, 2 * STRIP - MARGIN, STRIP - MARGIN)
        a, b, c, d = [pltpu.roll(v, shift % LANES, 1) for v, shift in zip(planes[n : n + 4], shifts)]
        packed += [jnp.where(lanes < (3 - k) * STRIP, v, w) for k, (v, w) in enumerate(((a, b), (b, c), (c, d)))]
    return packed


def unpack(packed):
    lanes = lane_index(packed[0].shape)
    cells = (lanes >= MARGIN) & (lanes < RIGHT)
    planes = []
    for n in range(0, len(packed), 3):
        first, second, third = packed[n : n + 3]
        b = jnp.where(lanes >= 3 * STRIP, first, second)
        c = jnp.where(lanes >= 2 * STRIP, second, third)
        shifts = (MARGIN, MARGIN - 3 * STRIP, MARGIN - 2 * STRIP, MARGIN - STRIP)
        moved = [pltpu.roll(v, shift % LANES, 1) for v, shift in zip((first, b, c, third), shifts)]
        planes += [jnp.where(cells, v, 0.0) for v in moved]
    return planes


def store(target, planes):
    for n, value in enumerate(planes):
        target[pl.ds(n * KEEP, KEEP), :] = value


def meet(stage, image, tiles, half, wanted, target, side):
    pairs, slots = wanted
    fill(stage, image, tiles, half, pairs, slots)
    at_left = lax.axis_index("col") == 0

    def border(slot):
        here, there = image(slot, tiles - 1), image(slot, 0)
        return [
            [jnp.where(at_left, pltpu.roll(v, STRIP, 1), w) for v, w in zip(p, q)]
            for p, q in zip(here, there)
        ]

    bordered = {slot: border(slot) for slot in range(-2, 4)}
    values = [v for a, b in CANDIDATES for v in product(bordered[a], bordered[b])]
    values += [power(bordered[slot]) for slot in range(-2, 4)]
    block = lane_index((half, LANES)) >> 5
    rows = pl.ds((2 * len(pairs) + len(slots)) * half, half)
    for tile in range(tiles):
        row = jnp.zeros((half, LANES), F32)
        for k, value in enumerate(values[4 * tile : 4 * tile + 4]):
            row = jnp.where(block == k, pltpu.roll(value, STRIP * k, 1) if k else value, row)
        stage[rows, pl.ds(tile * LANES, LANES)] = row
    means = split_dot(stage[...], looks_table(tiles * LANES))
    count = 2 * len(pairs) + len(slots)
    if wanted is GOING:
        store(target, pack([means[n * half : (n + 1) * half] for n in range(count)]))
    else:
        target[...] = means[: count * half]
    side[...] = means[count * half :]


ALL = (HELD + SENT, (0, 1, 2, 3))
GOING = (SENT, (2, 3))


def near_kernel(*refs):
    own, (held, sent, side, stage, means) = refs[0], refs[-5:]
    tiles, half = own.shape[0], own.shape[3] // 2
    before, after = [refs[1 + n * tiles : 1 + (n + 1) * tiles] for n in range(2)]

    @pl.when(lax.axis_index("date") % RUN < RUN - 1)
    def _():
        image = reader(own, {-1: (before, None, None), 1: (after, None, None)})
        meet(stage, image, tiles, half, ALL, means, side)
        share(means, half, held, sent)


def share(means, half, held, sent):
    kept, going = 2 * len(HELD) * half, 2 * len(SENT) * half
    held[pl.ds(0, kept), :] = means[pl.ds(0, kept), :]
    held[pl.ds(kept, 4 * half), :] = means[pl.ds(kept + going, 4 * half), :]
    starts = [kept + n * half for n in range(2 * len(SENT))]
    starts += [kept + going + n * half for n in (2, 3)]
    store(sent, pack([means[pl.ds(start, half), :] for start in starts]))


def end_kernel(run, own, before, after, *refs):
    count = 2 if run == 0 else 4
    outs, (stage, mine, near, arrived) = refs[-4 - count : -4], refs[-4:]
    tiles, half = own.shape[0], own.shape[3] // 2

    @pl.when(lax.axis_index("date") % RUN == run)
    def _():
        copies = [pltpu.make_async_copy(own, mine, arrived.at[0, 0])]
        for n, source in enumerate((before, after)):
            for tile in range(tiles):
                lanes = pl.ds(tile * LANES, LANES)
                copies.append(
                    pltpu.make_async_copy(source.at[:, :, :, lanes], near.at[n, tile], arrived.at[n + 1, tile])
                )
        for copy in copies:
            copy.start()
        for copy in copies:
            copy.wait()
        blocks = [[near.at[n, tile] for tile in range(tiles)] for n in range(2)]
        image = reader(mine, {-1: (blocks[0], None, None), 1: (blocks[1], None, None)})
        if run == 0:
            sent, side = outs
            side[pl.ds(half, side.shape[0] - half), :] = jnp.zeros((side.shape[0] - half, LANES), F32)
            meet(stage, image, tiles, half, GOING, sent, side.at[pl.ds(0, half), :])
        else:
            held, sent, side, means = outs
            meet(stage, image, tiles, half, ALL, means, side)
            share(means, half, held, sent)


def planes_of(rows, *counts):
    return tuple(jax.ShapeDtypeStruct((count * rows // 2, LANES), F32) for count in counts)


STAYING, LEAVING = 2 * len(HELD) + 4, 2 * len(SENT) + 2
PACKED = LEAVING * 3 // 4
BOTH = 2 * len(HELD + SENT) + 4


def at_end(run, own, before, after, *behind):
    rows, cols = after.shape[2:]
    half, tiles = rows // 2, cols // LANES
    outs = (PACKED, PACKED) if run == 0 else (STAYING, PACKED, 1)
    total = LEAVING if run == 0 else BOTH
    scratch = [
        pltpu.VMEM(((total + 1) * half, cols), F32),
        pltpu.VMEM(own.shape, F32),
        pltpu.VMEM((2,) + own.shape, F32),
        pltpu.SemaphoreType.DMA((3, tiles)),
    ]
    return call(
        functools.partial(end_kernel, run),
        planes_of(rows, *outs),
        3 + len(behind),
        ([] if run == 0 else [pltpu.VMEM((BOTH * half, LANES), F32)]) + scratch,
        [pl.BlockSpec(memory_space=pl.ANY)] * (3 + len(behind)),
    )(own, before, after, *behind)


def near(own, *images):
    rows, cols = images[0].shape[2:]
    half = rows // 2
    whole = lambda shape: pl.BlockSpec(shape, lambda i: (0,) * len(shape))
    outs = planes_of(rows, STAYING, PACKED, 1)
    return pl.pallas_call(
        near_kernel,
        grid=(1,),
        out_shape=outs,
        in_specs=[whole(own.shape)] + [spec for image in images for spec in tiled(image)],
        out_specs=tuple(whole(out.shape) for out in outs),
        scratch_shapes=[pltpu.VMEM(((BOTH + 1) * half, cols), F32), pltpu.VMEM((BOTH * half, LANES), F32)],
        compiler_params=pltpu.CompilerParams(vmem_limit_bytes=32 * 1024 * 1024),
    )(own, *[image for image in images for _ in range(cols // LANES)])


def arrived_kernel(side, back, new_side, new_back):
    new_side[...] = side[pl.ds(0, new_side.shape[0]), :]
    new_back[...] = back[...]


def merge_kernel(side, back, low_side, low_back, new_side, new_back):
    from_low = lax.axis_index("date") % RUN == RUN - 1
    new_side[...] = jnp.where(from_low, low_side[pl.ds(0, side.shape[0]), :], side[...])
    new_back[...] = jnp.where(from_low, low_back[...], back[...])


def rims_kernel(
    slots,
    held,
    last_held,
    side,
    back,
    high_side,
    high_back,
    picked,
    chip,
    across,
    every,
):
    at_left = lax.axis_index("col") == 0
    lanes = lane_index((KEEP, LANES))
    edge = jnp.where(at_left, RIGHT, 0)
    margin = (lanes >= edge) & (lanes < edge + MARGIN)
    place = lax.axis_index("date") % RUN
    from_low, from_high = place == RUN - 1, place == RUN - 2
    columns = jnp.where(from_high, high_side[...], side[...])
    rows = [pl.ds(n * KEEP, KEEP) for n in range(back.shape[0] // KEEP)]
    returned = unpack([jnp.where(from_high, high_back[r, :], back[r, :]) for r in rows])
    held_at, back_at = 0, 0
    for n in range(PLANES):
        pair = n // 2
        from_back = pair in (3, 6, 7) or n >= PLANES - 2
        if from_back:
            value, back_at = returned[back_at], back_at + 1
        else:
            rows = pl.ds(held_at * KEEP, KEEP)
            value, held_at = jnp.where(from_low, last_held[rows, :], held[rows, :]), held_at + 1
        here = MARGIN + MARGIN * n
        right = pltpu.roll(columns, (RIGHT - here) % LANES, 1)
        left = pltpu.roll(columns, -here % LANES, 1)
        every[pl.ds(n * KEEP, KEEP), :] = jnp.where(margin, jnp.where(at_left, right, left), value)

    even = lax.axis_index("row") % 2 == 0
    plane = lambda n: every[pl.ds(n * KEEP, KEEP), :]
    chosen = []
    for date in range(2):
        for link in range(LINKS):
            slot = jnp.broadcast_to(slots[pl.ds(LINKS * date + link, 1), :], (KEEP, LANES))
            triples = [
                (plane(2 * (3 * date + n - 1)), plane(2 * (3 * date + n - 1) + 1), plane(PLANES - 6 + n))
                for n in range(date + 1, date + 5)
            ]
            values = triples[0]
            for n, triple in zip(range(date + 2, date + 5), triples[1:]):
                values = [jnp.where(slot == n, v, w) for v, w in zip(triple, values)]
            chosen += values
    chosen += [plane(PLANES - 6 + date) for date in range(2)]
    for n, value in enumerate(chosen):
        picked[pl.ds(n * KEEP, KEEP), :] = value
        top, bottom = value[:MARGIN], value[KEEP - MARGIN :]
        chip[pl.ds(MARGIN * n, MARGIN), :] = jnp.where(even, bottom, top)
        across[pl.ds(MARGIN * n, MARGIN), :] = jnp.where(even, top, bottom)


@functools.lru_cache(None)
def tables():
    blocks = LANES // PATCH
    n = np.arange(PATCH)
    angle = 2.0 * np.pi * (np.outer(n, n) % PATCH) / PATCH
    cosine, sine = np.cos(angle), np.sin(angle)
    forward = np.zeros((LANES, 2 * LANES))
    spread = np.zeros((LANES, 2 * LANES))
    inverse = np.zeros((LANES, 2 * LANES))
    for b in range(blocks):
        f = slice(b * PATCH, (b + 1) * PATCH)
        x = slice(b * KEEP, b * KEEP + PATCH)
        o = slice(b * KEEP, (b + 1) * KEEP)
        kept = slice(MARGIN, MARGIN + KEEP)
        forward[x, f] = cosine
        forward[x, LANES + b * PATCH : LANES + (b + 1) * PATCH] = -sine
        inverse[f, o] = cosine[:, kept] / PATCH
        inverse[f, LANES + b * KEEP : LANES + (b + 1) * KEEP] = sine[:, kept] / PATCH
        near = (n[:, None] - n[None, :]) % PATCH
        spread[f, f] = (near == 0) | (near == 1) | (near == PATCH - 1)
        spread[f, LANES + b * PATCH : LANES + (b + 1) * PATCH] = 1.0
    down = np.block([[cosine, sine], [-sine, cosine]])
    kept = slice(MARGIN, MARGIN + KEEP)
    up = np.block([[cosine[kept], -sine[kept]], [sine[kept], cosine[kept]]]) / PATCH

    def thrice(table, axis):
        high = table.astype(np.float32).astype(BF16)
        low = (table - high.astype(np.float64)).astype(np.float32).astype(BF16)
        return np.concatenate([high, low, high], axis=axis)

    twice = np.concatenate([spread, spread], axis=0).astype(np.float32).astype(BF16)
    return [thrice(forward, 0), twice, thrice(inverse, 0), thrice(down, 1), thrice(up, 1)]


def parts(values):
    high = values.astype(BF16)
    return high, (values - high.astype(F32)).astype(BF16)


def narrow_dot(a, b):
    return jnp.dot(a, b, preferred_element_type=F32)


def right_dot(values, table):
    high, low = parts(values)
    return narrow_dot(jnp.concatenate([high, high, low], axis=1), table)


def left_dot(table, values):
    high, low = parts(values)
    return narrow_dot(table, jnp.concatenate([high, high, low], axis=0))


def sum_dot(values, table):
    return narrow_dot(jnp.concatenate(parts(values), axis=1), table)


def filter_kernel(picked, across, chip, forward, spread, inverse, down, up, filtered, coherent, pad):
    even = lax.axis_index("row") % 2 == 0
    pairs = 2 * LINKS
    for n in range(3 * pairs + 2):
        near, far = chip[pl.ds(MARGIN * n, MARGIN), :], across[pl.ds(MARGIN * n, MARGIN), :]
        pad[n, pl.ds(0, MARGIN), :] = jnp.where(even, far, near)
        pad[n, pl.ds(MARGIN, KEEP), :] = picked[pl.ds(n * KEEP, KEEP), :]
        pad[n, pl.ds(MARGIN + KEEP, MARGIN), :] = jnp.where(even, near, far)

    def box(value):
        rows = value[3 : 3 + KEEP] + value[4 : 4 + KEEP] + value[5 : 5 + KEEP]
        total = pltpu.roll(rows, LANES - 3, 1) + pltpu.roll(rows, LANES - 4, 1) + pltpu.roll(rows, LANES - 5, 1)
        return total * (1.0 / 9.0)

    wide = coherent.shape[-1]
    firsts = [box(pad[3 * pairs + date]) for date in range(2)]
    for p in range(pairs):
        real, imag, second = [box(pad[3 * p + k]) for k in range(3)]
        factor = lax.rsqrt(firsts[p // LINKS] * second + 1e-06)
        coherent[p // LINKS, p % LINKS, 0] = (real * factor)[:, :wide]
        coherent[p // LINKS, p % LINKS, 1] = (imag * factor)[:, :wide]

    reals = jnp.concatenate([pad[3 * p] for p in range(pairs)], axis=0)
    imags = jnp.concatenate([pad[3 * p + 1] for p in range(pairs)], axis=0)
    size = pairs * PATCH
    across_cols = right_dot(jnp.concatenate([reals, imags], axis=0), forward[...])
    col_real = across_cols[:size, :LANES] - across_cols[size:, LANES:]
    col_imag = across_cols[size:, :LANES] + across_cols[:size, LANES:]
    rows_of = lambda v, p, count: v[p * count : (p + 1) * count]
    stacked = jnp.concatenate(
        [
            jnp.concatenate([rows_of(col_real, p, PATCH), rows_of(col_imag, p, PATCH)], axis=0)
            for p in range(pairs)
        ],
        axis=1,
    )
    spectrum = left_dot(down[...], stacked)
    real, imag = spectrum[:PATCH], spectrum[PATCH:]
    power = real * real + imag * imag
    lanes_of = lambda v, p: v[:, p * LANES : (p + 1) * LANES]
    tall = lambda v: jnp.concatenate([lanes_of(v, p) for p in range(pairs)], axis=0)
    sums = sum_dot(tall(power), spread[...])
    weights = []
    for p in range(pairs):
        near = rows_of(sums, p, PATCH)[:, :LANES]
        level = jnp.sum(rows_of(sums, p, PATCH)[:, LANES:], axis=0, keepdims=True) * (1.0 / (PATCH * PATCH))
        smooth = (near + pltpu.roll(near, 1, 0) + pltpu.roll(near, PATCH - 1, 0)) * (1.0 / 9.0)
        weights.append(jnp.sqrt(jnp.sqrt(smooth + level + 1e-06)))
    totals = sum_dot(jnp.concatenate(weights, axis=0), spread[:, LANES:])
    scaled = []
    for p in range(pairs):
        total = jnp.sum(rows_of(totals, p, PATCH), axis=0, keepdims=True)
        scaled.append(weights[p] * ((PATCH * PATCH) / total))
    weight = jnp.concatenate(scaled, axis=1)
    lifted = left_dot(up[...], jnp.concatenate([real * weight, imag * weight], axis=0))
    low, high = lifted[:KEEP], lifted[KEEP:]
    size = pairs * KEEP
    result = right_dot(jnp.concatenate([tall(low), tall(high)], axis=0), inverse[...])
    out_real = result[:size, :LANES] - result[size:, LANES:]
    out_imag = result[size:, :LANES] + result[:size, LANES:]
    for p in range(pairs):
        filtered[p // LINKS, p % LINKS, 0] = rows_of(out_real, p, KEEP)[:, :wide]
        filtered[p // LINKS, p % LINKS, 1] = rows_of(out_imag, p, KEEP)[:, :wide]


def body(images, secondaries):
    rows, cols = images.shape[2:]
    cells_down, cells_along = rows // 2, cols // 8
    dates, count = lax.axis_size("date"), lax.axis_size("row")
    inner = lambda steps: [(d, d + steps) for d in range(dates) if 0 <= d % RUN + steps < RUN]
    outer = lambda steps: [(d, (d + steps) % dates) for d in range(dates) if not 0 <= d % RUN + steps < RUN]
    along = lambda value, pairs: lax.ppermute(value, "date", pairs)
    across = lambda value, pairs: lax.ppermute(
        value, ("date", "col"), [(2 * d + c, 2 * e + (c ^ 1)) for d, e in pairs for c in range(2)]
    )
    up_from = lambda wanted: [(d, d + 1) for d in range(dates) if wanted(d % RUN)]
    after, before = along(images, inner(-1)), along(images, up_from(lambda n: n < RUN - 2))
    after_wrap, before_wrap = along(images, outer(-1)), along(images, outer(1))
    before_last = along(images, up_from(lambda n: n == RUN - 2))
    own, slots = kept(images, secondaries)
    step = lambda wanted: [(d, (d - 1) % dates) for d in range(dates) if wanted(d % RUN)]
    middle, low, high = step(lambda n: 0 < n < RUN - 1), step(lambda n: n == 0), step(lambda n: n == RUN - 1)
    held, sent, side = near(own, before, after)
    side, back = across(side, middle), along(sent, middle)
    sent, low_side = at_end(0, own, before_wrap, after, side, before)
    formed = low_side
    low_side, low_back = across(low_side, low), along(sent, low)
    last_held, sent, high_side = at_end(RUN - 1, own, before_last, after_wrap, formed)
    high_side, high_back = across(high_side, high), along(sent, high)
    side, back = call(arrived_kernel, planes_of(rows, 1, PACKED), 2)(side, back)
    side, back = call(merge_kernel, planes_of(rows, 1, PACKED), 4)(side, back, low_side, low_back)

    planes = 3 * 2 * LINKS + 2
    rim = jax.ShapeDtypeStruct((planes * MARGIN, LANES), F32)
    every = pltpu.VMEM((PLANES * cells_down, LANES), F32)
    picked = jax.ShapeDtypeStruct((planes * cells_down, LANES), F32)
    picked, chip, across = call(rims_kernel, (picked, rim, rim), 7, [every])(
        slots, held, last_held, side, back, high_side, high_back
    )
    chip = lax.ppermute(chip, "row", [(i, i ^ 1) for i in range(count)])
    across = lax.ppermute(across, "row", [(i, ((i + 1) ^ 1) - 1) for i in range(1, count - 1)])
    out = jax.ShapeDtypeStruct((2, LINKS, 2, cells_down, cells_along), F32)
    return call(filter_kernel, (out, out), 8, [pltpu.VMEM((planes, PATCH, LANES), F32)])(
        picked, across, chip, *tables()
    )


def solution(mesh):
    in_specs = (P("date", None, "row", "col"), P("date", None))
    out_specs = (P("date", None, None, "row", "col"), P("date", None, None, "row", "col"))
    return jax.shard_map(body, mesh=mesh, in_specs=in_specs, out_specs=out_specs, check_vma=False)
```
